128 devices in a mesh: grp: 16 (over z_lo, x, core), vocab: 8 (over y, z_hi).
Axes of the slice: x: 4, y: 4, z: 4 (z_hi: 2, z_lo: 2; z = z_hi * 2 + z_lo), core: 2. Of those that a mesh axis runs over, the one named last changes fastest.
Arguments:
- embedded: bfloat16 [512, 4, 5120], P('grp'), may hold values from -6 to 6
- attn_gain: float32 [5120], replicated, may hold values from 0.1 to 1.9
- query_weight: bfloat16 [5120, 4096], P(None, 'vocab'), may hold values from -0.078125 to 0.078125
- key_weight: bfloat16 [5120, 1024], P(None, 'vocab'), may hold values from -0.3125 to 0.3125
- value_weight: bfloat16 [5120, 1024], P(None, 'vocab'), may hold values from -0.078125 to 0.078125
- out_weight: bfloat16 [4096, 5120], P('vocab'), may hold values from -0.75 to 0.75
- final_gain: float32 [5120], replicated, may hold values from 0.5 to 1.5
- head_weight: bfloat16 [5120, 81920], P(None, ('grp', 'vocab')), may hold values from -3 to 3
- prefix_keys: bfloat16 [16, 8, 2048, 128], P('grp', 'vocab'), may hold values from -150 to 150
- prefix_values: bfloat16 [16, 8, 2048, 128], P('grp', 'vocab'), may hold values from -6 to 6
- sample_prompt: int32 [512], P('grp'), may hold values from 0 to 15, as said below
Outputs:
- log_probs: float32 [512, 4, 81920], P(None, None, ('grp', 'vocab'))
The draws below stay inside these ranges and needn't reach their ends.
Inputs may be any that keep to these rules, and one draw needn't show every extreme that they name: `sample_prompt`: each device's aligned block of 32 samples holds exactly 2 samples of every one of the 16 prompts, in a drawn order.
All inputs are finite; a program needn't handle non-finite values.
Results may differ from the reference program's by a relative error of at most 0.0029.
The reference program's roundings to bfloat16 on the way count: a program that leaves them out, or rounds other values in their place, can miss the bound.
Values may be sent and summed in bfloat16 or wider, within the bound.
No kernel may reach another device: no remote copies, remote signals or barrier semaphores. Data moves between devices by JAX's collectives and lax.ppermute only.
A program may use at most 128 MiB of HBM per device.

```python
import math
import jax
import jax.numpy as jnp
from jax import lax

D = 5120
HEAD = 128
KV_HEADS = 8
QPG = 4
PREFIX = 2048
PER_PROMPT = 2
STEPS = 4
PROMPTS = 16
SAMP_DEV = 32
SAMPLES = 512
VOCAB = 81920


def draw_sample_prompt(key, part):
    key = jax.random.fold_in(key, 11)
    blocks = SAMPLES // SAMP_DEV
    base = jnp.arange(SAMP_DEV, dtype=jnp.int32) // PER_PROMPT
    tiled = jnp.broadcast_to(base[None, :], (blocks, SAMP_DEV))
    mixed = jax.random.permutation(key, tiled, axis=1, independent=True)
    return mixed.reshape(SAMPLES).astype(jnp.int32)


def draw_prefix_keys(key, part):
    key = jax.random.fold_in(key, 5)
    key_base = jax.random.fold_in(key, 0)
    full_shape = (PROMPTS, KV_HEADS, PREFIX, HEAD)
    values = 1.5 * jnp.clip(jax.random.normal(key_base, full_shape, jnp.float32), -6.0, 6.0)
    return jnp.clip(values, -150.0, 150.0).astype(jnp.bfloat16)


def draw_head_weight(key, part):
    key = jax.random.fold_in(key, 7)
    key_base = jax.random.fold_in(key, 0)
    full_shape = (D, VOCAB)
    spread = 3.0 / math.sqrt(D)
    values = jnp.clip(jax.random.normal(key_base, full_shape, jnp.float32), -6.0, 6.0) * spread
    return jnp.clip(values, -3.0, 3.0).astype(jnp.bfloat16)


def shard_levels(stream_key, dims, shards, low, top_value):
    def one(axis_at, blocks):
        draws = jax.random.uniform(jax.random.fold_in(jax.random.fold_in(stream_key, 6), axis_at), (blocks,), jnp.float32, low / len(shards), top_value / len(shards))
        return jnp.repeat(jnp.exp(draws), dims[axis_at] // blocks).reshape((-1,) + (1,) * (len(dims) - axis_at - 1))

    level = one(*shards[0])
    for cut in shards[1:]:
        level = level * one(*cut)
    return level


def bell_draw(own_key, dims, deviation, bound, shards=(), kind=jnp.bfloat16):
    drawn = jax.random.normal(own_key, dims, jnp.float32) * deviation
    if len(shards) > 0:
        drawn = shard_levels(own_key, dims, shards, -0.22, 0.18) * drawn
    return jnp.clip(drawn, min=-bound, max=bound).astype(kind)


def setup_inputs(seed: int = 0) -> dict:
    key_of = jax.random.split(jax.random.key(seed), 12)
    embedded = bell_draw(key_of[0], (SAMPLES, STEPS, D), 1.0, 6.0, ((0, 16),))
    attn_gain = jnp.clip(1.0 + 0.18 * jax.random.normal(key_of[1], (D,), jnp.float32), 0.1, 1.9)
    query_weight = bell_draw(key_of[2], (D, KV_HEADS * QPG * HEAD), D ** -0.5, 0.078125, ((1, 8),))
    key_weight = bell_draw(key_of[3], (D, KV_HEADS * HEAD), (D // 16) ** -0.5, 0.3125, ((1, 8),))
    value_weight = bell_draw(key_of[4], (D, KV_HEADS * HEAD), D ** -0.5, 0.078125, ((1, 8),))
    out_weight = bell_draw(key_of[5], (KV_HEADS * QPG * HEAD, D), (max(1, KV_HEADS * QPG * HEAD // 64)) ** -0.5, 0.75, ((0, 8),))
    final_gain = jnp.clip(1.0 + 0.1 * jax.random.normal(key_of[6], (D,), jnp.float32), 0.5, 1.5)
    head_weight = draw_head_weight(jax.random.fold_in(key_of[11], 71), 0)
    prefix_keys = draw_prefix_keys(jax.random.fold_in(key_of[11], 71), 0)
    prefix_values = bell_draw(key_of[9], (PROMPTS, KV_HEADS, PREFIX, HEAD), 1.0, 6.0, ((0, 16), (1, 8)))
    sample_prompt = draw_sample_prompt(jax.random.fold_in(key_of[11], 71), 0)
    return {"embedded": embedded, "attn_gain": attn_gain, "query_weight": query_weight, "key_weight": key_weight, "value_weight": value_weight, "out_weight": out_weight, "final_gain": final_gain, "head_weight": head_weight, "prefix_keys": prefix_keys, "prefix_values": prefix_values, "sample_prompt": sample_prompt}


def rms_scale(rows, gain):
    mean_sq = lax.optimization_barrier(jnp.mean(rows * rows, axis=-1, keepdims=True))
    return rows * lax.rsqrt(mean_sq + 1e-06) * gain

def softmax_parts(scores, value_rows, value_form):
    peaks = lax.optimization_barrier(jnp.max(scores, axis=-1))
    powers = jnp.exp(scores - peaks[..., None])
    totals = lax.optimization_barrier(jnp.sum(powers, axis=-1))
    rounded = lax.optimization_barrier(powers.astype(jnp.bfloat16)).astype(jnp.float32)
    weighted = jnp.einsum(value_form, rounded, value_rows)
    return (peaks, totals, weighted)

def reference(embedded, attn_gain, query_weight, key_weight, value_weight, out_weight, final_gain, head_weight, prefix_keys, prefix_values, sample_prompt):
    score_scale = 1.0 / HEAD ** 0.5
    flat_rows = embedded.reshape(SAMPLES * STEPS, D)
    normed_input = rms_scale(flat_rows.astype(jnp.float32), attn_gain).astype(jnp.bfloat16)
    queries = jnp.dot(normed_input, query_weight, preferred_element_type=jnp.float32).astype(jnp.bfloat16)
    new_keys = jnp.dot(normed_input, key_weight, preferred_element_type=jnp.float32).astype(jnp.bfloat16)
    new_values = jnp.dot(normed_input, value_weight, preferred_element_type=jnp.float32).astype(jnp.bfloat16)
    queries = queries.reshape(SAMPLES, STEPS, KV_HEADS, QPG, HEAD).astype(jnp.float32)
    new_keys = new_keys.reshape(SAMPLES, STEPS, KV_HEADS, HEAD).astype(jnp.float32)
    new_values = new_values.reshape(SAMPLES, STEPS, KV_HEADS, HEAD).astype(jnp.float32)

    def one_sample(sample_item):
        query_rows, prompt = sample_item
        key_rows = lax.dynamic_index_in_dim(prefix_keys, prompt, 0, keepdims=False).astype(jnp.float32)
        value_rows = lax.dynamic_index_in_dim(prefix_values, prompt, 0, keepdims=False).astype(jnp.float32)
        scores = jnp.einsum('tjgh,jlh->tjgl', query_rows, key_rows) * score_scale
        return softmax_parts(scores, value_rows, 'tjgl,jlh->tjgh')
    prefix_peak, prefix_total, prefix_sum = lax.map(one_sample, (queries, sample_prompt.astype(jnp.int32)))
    scores = jnp.einsum('stjgh,sujh->stjgu', queries, new_keys) * score_scale
    step_index = jnp.arange(STEPS)
    causal = step_index[:, None] >= step_index[None, :]
    scores = jnp.where(causal[None, :, None, None, :], scores, -1e+30)
    new_peak, new_total, new_sum = softmax_parts(scores, new_values, 'stjgu,sujh->stjgh')
    joint_peak = jnp.maximum(prefix_peak, new_peak)
    prefix_factor = jnp.exp(prefix_peak - joint_peak)
    new_factor = jnp.exp(new_peak - joint_peak)
    numerator = prefix_sum * prefix_factor[..., None] + new_sum * new_factor[..., None]
    denominator = prefix_total * prefix_factor + new_total * new_factor
    attended = (numerator / denominator[..., None]).astype(jnp.bfloat16)
    attended = attended.reshape(SAMPLES * STEPS, KV_HEADS * QPG * HEAD)
    hidden = flat_rows.astype(jnp.float32) + jnp.dot(attended, out_weight, preferred_element_type=jnp.float32)
    normed = rms_scale(hidden, final_gain).astype(jnp.bfloat16)
    logits = jnp.dot(normed, head_weight, preferred_element_type=jnp.float32)
    peaks = lax.optimization_barrier(jnp.max(logits, axis=-1, keepdims=True))
    log_total = peaks + jnp.log(lax.optimization_barrier(jnp.sum(jnp.exp(logits - peaks), axis=-1, keepdims=True)))
    return (logits - log_total).reshape(SAMPLES, STEPS, VOCAB)
```

```python
import jax
import jax.numpy as jnp
import numpy as np
from jax import lax
from jax.sharding import PartitionSpec as P

BOTH = ("grp", "vocab")
RING = 4
PIECES = ((0, 1664), (1664, 3456), (3456, 5120))
ORDERS = ("xyz", "yzx", "zxy")


def place_of(flat):
    grp, vocab = divmod(flat, 8)
    z_lo, rest = divmod(grp, 8)
    x, core = divmod(rest, 2)
    y, z_hi = divmod(vocab, 2)
    return {"x": x, "y": y, "z": z_hi * 2 + z_lo, "core": core}


def flat_of(at):
    grp = (at["z"] % 2) * 8 + at["x"] * 2 + at["core"]
    return grp * 8 + at["y"] * 2 + at["z"] // 2


def ring_pairs(axis):
    pairs = []
    for source in range(128):
        at = place_of(source)
        at[axis] = (at[axis] + (1 if at["core"] == 0 else -1)) % RING
        pairs.append((source, flat_of(at)))
    return pairs


def core_pairs():
    pairs = []
    for source in range(128):
        at = place_of(source)
        at["core"] = 1 - at["core"]
        pairs.append((source, flat_of(at)))
    return pairs


STEP = {axis: ring_pairs(axis) for axis in "xyz"}
SWAP = core_pairs()


def swap_cores(block):
    return lax.ppermute(block, BOTH, SWAP)


def ring_gather(blocks):
    held = list(blocks)
    for stage in range(3):
        rounds = [[part] for part in held]
        for _ in range(RING - 1):
            for k, order in enumerate(ORDERS):
                rounds[k].append(lax.ppermute(rounds[k][-1], BOTH, STEP[order[stage]]))
        held = [jnp.stack(parts) for parts in rounds]
    return held


def rms_scale(rows, gain):
    mean_sq = jnp.mean(rows * rows, axis=-1, keepdims=True)
    return rows * lax.rsqrt(mean_sq + 1e-06) * gain


def softmax_parts(scores, value_rows, value_form):
    peaks = jnp.max(scores, axis=-1)
    powers = jnp.exp(scores - peaks[..., None])
    totals = jnp.sum(powers, axis=-1)
    weighted = jnp.einsum(
        value_form, powers.astype(jnp.bfloat16), value_rows, preferred_element_type=jnp.float32
    )
    return (peaks, totals, weighted)


def log_sum(values, axis):
    top = jnp.max(values, axis=axis, keepdims=True)
    return jnp.squeeze(top, axis) + jnp.log(jnp.sum(jnp.exp(values - top), axis=axis))


def spread(values, axis):
    copies = lax.axis_size(axis)
    return lax.all_to_all(
        jnp.broadcast_to(values[None], (copies,) + values.shape), axis, 0, 0, tiled=True
    )


def on_device(
    embedded,
    attn_gain,
    query_weight,
    key_weight,
    value_weight,
    out_weight,
    final_gain,
    head_weight,
    prefix_keys,
    prefix_values,
    sample_prompt,
):
    samples, steps, width = embedded.shape
    head = prefix_keys.shape[3]
    groups = query_weight.shape[1] // head
    rows = samples * steps
    scale = 1.0 / head**0.5
    other_weight = swap_cores(head_weight)

    flat_rows = embedded.reshape(rows, width)
    normed_input = rms_scale(flat_rows.astype(jnp.float32), attn_gain).astype(jnp.bfloat16)
    project = lambda w: jnp.dot(normed_input, w, preferred_element_type=jnp.float32).astype(
        jnp.bfloat16
    )
    projected = jnp.concatenate(
        [project(query_weight), project(key_weight), project(value_weight)], axis=1
    )

    same = sample_prompt[:, None] == sample_prompt[None, :]
    earlier = jnp.arange(samples)[:, None] > jnp.arange(samples)[None, :]
    slot = sample_prompt * 2 + jnp.sum(same & earlier, axis=1, dtype=jnp.int32)
    row_slot = (slot[:, None] * steps + jnp.arange(steps, dtype=jnp.int32)[None, :]).reshape(rows)
    to_sorted = (row_slot[None, :] == jnp.arange(rows, dtype=jnp.int32)[:, None]).astype(jnp.bfloat16)
    sorted_rows = jnp.dot(to_sorted, projected, preferred_element_type=jnp.float32).astype(
        jnp.bfloat16
    )
    local = lax.all_to_all(sorted_rows, "grp", 0, 0, tiled=True)

    cut = groups * head
    queries = local[:, :cut].reshape(samples, steps, groups, head)
    new_keys = local[:, cut : cut + head].reshape(samples, steps, head)
    new_values = local[:, cut + head :].reshape(samples, steps, head)
    scores = (
        jnp.einsum("stgh,lh->stgl", queries, prefix_keys[0, 0], preferred_element_type=jnp.float32)
        * scale
    )
    prefix_peak, prefix_total, prefix_sum = softmax_parts(
        scores, prefix_values[0, 0], "stgl,lh->stgh"
    )
    scores = jnp.einsum("stgh,suh->stgu", queries, new_keys, preferred_element_type=jnp.float32) * scale
    step_index = jnp.arange(steps)
    causal = step_index[:, None] >= step_index[None, :]
    scores = jnp.where(causal[None, :, None, :], scores, -1e30)
    new_peak, new_total, new_sum = softmax_parts(scores, new_values, "stgu,suh->stgh")
    peak = jnp.maximum(prefix_peak, new_peak)
    prefix_factor = jnp.exp(prefix_peak - peak)
    new_factor = jnp.exp(new_peak - peak)
    numerator = prefix_sum * prefix_factor[..., None] + new_sum * new_factor[..., None]
    denominator = prefix_total * prefix_factor + new_total * new_factor
    attended = (numerator / denominator[..., None]).astype(jnp.bfloat16).reshape(rows, cut)

    back = lax.all_to_all(attended, "grp", 0, 0, tiled=True)
    attended = jnp.dot(to_sorted.T, back, preferred_element_type=jnp.float32).astype(jnp.bfloat16)
    partial_heads = jnp.dot(attended, out_weight, preferred_element_type=jnp.float32)
    shares = lax.axis_size("vocab")
    mine = rows // shares
    arrived = lax.all_to_all(partial_heads, "vocab", 0, 0, tiled=True)
    summed = jnp.sum(arrived.reshape(shares, mine, width), axis=0)
    own_rows = lax.dynamic_slice_in_dim(flat_rows, lax.axis_index("vocab") * mine, mine, 0)
    normed = rms_scale(own_rows.astype(jnp.float32) + summed, final_gain).astype(jnp.bfloat16)

    gathered = ring_gather([normed[:, a:b] for a, b in PIECES])
    turned = (
        gathered[0],
        gathered[1].transpose(1, 2, 0, 3, 4),
        gathered[2].transpose(2, 0, 1, 3, 4),
    )
    plane = jnp.concatenate([t.reshape(64 * mine, t.shape[-1]) for t in turned], axis=1)
    logits = jnp.dot(plane, head_weight, preferred_element_type=jnp.float32)
    other_logits = jnp.dot(plane, other_weight, preferred_element_type=jnp.float32)
    crossed = swap_cores(other_logits)

    core = lax.axis_index("grp") % 2
    z = (lax.axis_index("vocab") % 2) * 2 + lax.axis_index("grp") // 8
    y = lax.axis_index("vocab") // 2
    x = (lax.axis_index("grp") // 2) % 4
    places = jnp.arange(4, dtype=jnp.int32)
    near = lambda c, at: jnp.where(c == 0, at - places, places - at) % 4
    find = lambda c: (
        near(c, z)[:, None, None] * 16 + near(c, y)[None, :, None] * 4 + near(c, x)[None, None, :]
    )

    local_sum = log_sum(jnp.concatenate([logits, other_logits], axis=1), 1)
    mine_order = find(core).reshape(64)
    local_sum = jnp.take(local_sum.reshape(64, mine), mine_order, axis=0)
    over_grp = spread(local_sum, "grp").reshape(8, 2, 64, mine)
    over_grp = log_sum(over_grp, 0)
    total = log_sum(spread(over_grp, "vocab").reshape(shares, 2, 64, mine), 0)

    def rearrange(blocks):
        return blocks.transpose((2, 4, 0, 3, 1) + tuple(range(5, blocks.ndim)))

    total = rearrange(total.reshape(2, 2, 2, 4, 4, mine))
    own_at = find(core).reshape(64)
    other_at = find(1 - core).reshape(64) + 64
    first = jnp.where(core == 0, own_at, other_at)
    second = jnp.where(core == 0, other_at, own_at)
    source = rearrange(jnp.stack([first, second]).reshape(2, 2, 2, 4, 4)).reshape(128)
    blocks = jnp.concatenate([logits, crossed]).reshape(128, mine, head_weight.shape[1])
    result = jnp.take(blocks, source, axis=0) - total.reshape(128, mine, 1)
    return result.reshape(-1, steps, head_weight.shape[1])


def solution(mesh):
    placed = (
        P("grp", None, None),
        P(),
        P(None, "vocab"),
        P(None, "vocab"),
        P(None, "vocab"),
        P("vocab", None),
        P(),
        P(None, ("grp", "vocab")),
        P("grp", "vocab", None, None),
        P("grp", "vocab", None, None),
        P("grp"),
    )
    return jax.shard_map(
        on_device,
        mesh=mesh,
        in_specs=placed,
        out_specs=P(None, None, ("grp", "vocab")),
        check_vma=False,
    )
```

```python
import jax
import jax.numpy as jnp
from jax import lax
from jax.experimental import pallas as pl
from jax.experimental.pallas import tpu as pltpu
from jax.sharding import PartitionSpec as P

BOTH = ("grp", "vocab")
RING = 4
PIECES = ((0, 1792), (1792, 3584), (3584, 5120))
ORDERS = ("xyz", "yzx", "zxy")


def place_of(flat):
    grp, vocab = divmod(flat, 8)
    z_lo, rest = divmod(grp, 8)
    x, core = divmod(rest, 2)
    y, z_hi = divmod(vocab, 2)
    return {"x": x, "y": y, "z": z_hi * 2 + z_lo, "core": core}


def flat_of(at):
    grp = (at["z"] % 2) * 8 + at["x"] * 2 + at["core"]
    return grp * 8 + at["y"] * 2 + at["z"] // 2


def ring_pairs(axis):
    pairs = []
    for source in range(128):
        at = place_of(source)
        at[axis] = (at[axis] + (1 if at["core"] == 0 else -1)) % RING
        pairs.append((source, flat_of(at)))
    return pairs


def swap_pairs(axis, distance, size):
    pairs = []
    for source in range(128):
        at = place_of(source)
        at[axis] = (at[axis] + distance) % size
        pairs.append((source, flat_of(at)))
    return pairs


STEP = {axis: ring_pairs(axis) for axis in "xyz"}
CORES = swap_pairs("core", 1, 2)
HALVES = swap_pairs("z", 2, RING)


def swap_cores(block):
    return lax.ppermute(block, BOTH, CORES)


def ring_gather(blocks):
    held = list(blocks)
    for stage in range(3):
        rounds = [[part] for part in held]
        for _ in range(RING - 1):
            for k, order in enumerate(ORDERS):
                rounds[k].append(lax.ppermute(rounds[k][-1], BOTH, STEP[order[stage]]))
        if stage < 2:
            held = [jnp.stack(parts) for parts in rounds]
    return rounds


def head_kernel(*refs):
    parts = (refs[0:4], refs[4:8], refs[8:12])
    own_w, other_w, own_out, other_out, sums, *work = refs[12:]
    lhs, weights, (total, lhs_sem, w_sem, out_sem) = work[0:3], work[3:6], work[6:]
    half = own_w.shape[1]

    def weight_copies(k):
        a, b = PIECES[k]
        rows = pl.ds(a, b - a)
        return [
            pltpu.make_async_copy(own_w.at[rows], weights[k].at[:, pl.ds(0, half)], w_sem.at[k, 0]),
            pltpu.make_async_copy(
                other_w.at[rows], weights[k].at[:, pl.ds(half, half)], w_sem.at[k, 1]
            ),
        ]

    def part_copies(k):
        return [
            pltpu.make_async_copy(parts[k][r], lhs[k].at[r], lhs_sem.at[k, r]) for r in range(RING)
        ]

    def out_copies(z):
        rows = pl.ds(z * 256, 256)
        return [
            pltpu.make_async_copy(total.at[rows, pl.ds(0, half)], own_out.at[rows], out_sem.at[z, 0]),
            pltpu.make_async_copy(
                total.at[rows, pl.ds(half, half)], other_out.at[rows], out_sem.at[z, 1]
            ),
        ]

    for k in range(3):
        for copy in part_copies(k) + weight_copies(k):
            copy.start()

    def rows_of(k, z):
        if k == 0:
            blocks = [lhs[0][z, y, x] for y in range(4) for x in range(4)]
        elif k == 1:
            blocks = [lhs[1][x, z, y] for y in range(4) for x in range(4)]
        else:
            blocks = [lhs[2][y, x, z] for y in range(4) for x in range(4)]
        return jnp.concatenate(blocks, axis=0)

    for k in range(3):
        for copy in part_copies(k) + weight_copies(k):
            copy.wait()

        def tile(z, carry, k=k):
            rows = pl.ds(pl.multiple_of(z * 256, 256), 256)
            fresh = jnp.dot(rows_of(k, z), weights[k][...], preferred_element_type=jnp.float32)
            if k > 0:
                fresh = total[rows] + fresh
            total[rows] = fresh
            if k == 2:
                for copy in out_copies(z):
                    copy.start()
                top = jnp.max(fresh, axis=1, keepdims=True)
                sums[rows] = top + jnp.log(jnp.sum(jnp.exp(fresh - top), axis=1, keepdims=True))
            return carry

        lax.fori_loop(0, RING, tile, 0)
    for z in range(RING):
        for copy in out_copies(z):
            copy.wait()


def head_logits(rounds, own_w, other_w, mine):
    half = own_w.shape[1]
    rows = 64 * mine
    anywhere = pl.BlockSpec(memory_space=pl.ANY)
    widths = [b - a for a, b in PIECES]
    return pl.pallas_call(
        head_kernel,
        out_shape=(
            jax.ShapeDtypeStruct((rows, half), jnp.float32),
            jax.ShapeDtypeStruct((rows, half), jnp.float32),
            jax.ShapeDtypeStruct((rows, 1), jnp.float32),
        ),
        in_specs=[anywhere] * 14,
        out_specs=(anywhere, anywhere, pl.BlockSpec(memory_space=pltpu.VMEM)),
        scratch_shapes=[pltpu.VMEM((4, 4, 4, mine, w), jnp.bfloat16) for w in widths]
        + [pltpu.VMEM((w, 2 * half), jnp.bfloat16) for w in widths]
        + [
            pltpu.VMEM((rows, 2 * half), jnp.float32),
            pltpu.SemaphoreType.DMA((3, RING)),
            pltpu.SemaphoreType.DMA((3, 2)),
            pltpu.SemaphoreType.DMA((RING, 2)),
        ],
        compiler_params=pltpu.CompilerParams(vmem_limit_bytes=52 * 2**20),
        name="head",
    )(*rounds[0], *rounds[1], *rounds[2], own_w, other_w)


def output_kernel(order, place, own, other, totals, out):
    pair = pl.program_id(0)
    y, z_hi = pair // 2, pair % 2
    core, x_here, y_here, z_here = place[0], place[1], place[2], place[3]
    for ref, plane in ((own, core), (other, 1 - core)):
        sign = 1 - 2 * plane
        away = lambda here, there: (sign * (here - there)) & 3
        for z_lo in range(2):
            for x in range(4):
                prompt = z_lo * 8 + x * 2 + plane
                block = ref[away(z_here, z_hi * 2 + z_lo), away(y_here, y), away(x_here, x)]
                block = block - totals[prompt, pair]
                for row in range(4):
                    near, which = divmod(row, 2)
                    to = order[(pair * 2 + near) * 32 + prompt * 2 + which]
                    out[near * 32 + to] = block[row * 4 : row * 4 + 4]


def ordered_output(order, place, own, other, totals):
    width = own.shape[-1]
    whole = lambda a: pl.BlockSpec(a.shape, lambda i, *_: (0,) * a.ndim)
    return pl.pallas_call(
        output_kernel,
        out_shape=jax.ShapeDtypeStruct((512, 4, width), jnp.float32),
        grid_spec=pltpu.PrefetchScalarGridSpec(
            num_scalar_prefetch=2,
            grid=(8,),
            in_specs=[whole(own), whole(other), whole(totals)],
            out_specs=pl.BlockSpec((64, 4, width), lambda i, *_: (i, 0, 0)),
        ),
        compiler_params=pltpu.CompilerParams(vmem_limit_bytes=52 * 2**20),
        name="output",
    )(order, place, own, other, totals)


def rms_scale(rows, gain):
    mean_sq = jnp.mean(rows * rows, axis=-1, keepdims=True)
    return rows * lax.rsqrt(mean_sq + 1e-06) * gain


def softmax_parts(scores, value_rows, value_form):
    peaks = jnp.max(scores, axis=-1)
    powers = jnp.exp(scores - peaks[..., None])
    totals = jnp.sum(powers, axis=-1)
    weighted = jnp.einsum(
        value_form, powers.astype(jnp.bfloat16), value_rows, preferred_element_type=jnp.float32
    )
    return (peaks, totals, weighted)


def log_sum(values, axis):
    top = jnp.max(values, axis=axis, keepdims=True)
    return jnp.squeeze(top, axis) + jnp.log(jnp.sum(jnp.exp(values - top), axis=axis))


def spread(values, axis):
    copies = lax.axis_size(axis)
    return lax.all_to_all(
        jnp.broadcast_to(values[None], (copies,) + values.shape), axis, 0, 0, tiled=True
    )


def on_device(
    embedded,
    attn_gain,
    query_weight,
    key_weight,
    value_weight,
    out_weight,
    final_gain,
    head_weight,
    prefix_keys,
    prefix_values,
    sample_prompt,
):
    samples, steps, width = embedded.shape
    head = prefix_keys.shape[3]
    groups = query_weight.shape[1] // head
    rows = samples * steps
    scale = 1.0 / head**0.5
    other_weight = swap_cores(head_weight)
    core = lax.axis_index("grp") % 2
    z_hi = lax.axis_index("vocab") % 2
    z = z_hi * 2 + lax.axis_index("grp") // 8
    y = lax.axis_index("vocab") // 2
    x = (lax.axis_index("grp") // 2) % 4
    shares = lax.axis_size("vocab")
    span = width // shares
    first_column = lax.axis_index("vocab") * span

    flat_rows = embedded.reshape(rows, width)
    normed_input = rms_scale(flat_rows.astype(jnp.float32), attn_gain).astype(jnp.bfloat16)
    project = lambda w: jnp.dot(normed_input, w, preferred_element_type=jnp.float32).astype(
        jnp.bfloat16
    )
    projected = jnp.concatenate(
        [
            project(query_weight),
            project(key_weight),
            project(value_weight),
            lax.dynamic_slice_in_dim(flat_rows, first_column, span, 1),
        ],
        axis=1,
    )

    same = sample_prompt[:, None] == sample_prompt[None, :]
    earlier = jnp.arange(samples)[:, None] > jnp.arange(samples)[None, :]
    slot = sample_prompt * 2 + jnp.sum(same & earlier, axis=1, dtype=jnp.int32)
    row_slot = (slot[:, None] * steps + jnp.arange(steps, dtype=jnp.int32)[None, :]).reshape(rows)
    to_sorted = (row_slot[None, :] == jnp.arange(rows, dtype=jnp.int32)[:, None]).astype(jnp.bfloat16)
    sorted_rows = jnp.dot(to_sorted, projected, preferred_element_type=jnp.float32).astype(
        jnp.bfloat16
    )
    local = lax.all_to_all(sorted_rows, "grp", 0, 0, tiled=True)

    cut = groups * head
    queries = local[:, :cut].reshape(samples, steps, groups, head)
    new_keys = local[:, cut : cut + head].reshape(samples, steps, head)
    new_values = local[:, cut + head : cut + 2 * head].reshape(samples, steps, head)
    scores = (
        jnp.einsum("stgh,lh->stgl", queries, prefix_keys[0, 0], preferred_element_type=jnp.float32)
        * scale
    )
    prefix_peak, prefix_total, prefix_sum = softmax_parts(
        scores, prefix_values[0, 0], "stgl,lh->stgh"
    )
    scores = jnp.einsum("stgh,suh->stgu", queries, new_keys, preferred_element_type=jnp.float32) * scale
    step_index = jnp.arange(steps)
    causal = step_index[:, None] >= step_index[None, :]
    scores = jnp.where(causal[None, :, None, :], scores, -1e30)
    new_peak, new_total, new_sum = softmax_parts(scores, new_values, "stgu,suh->stgh")
    peak = jnp.maximum(prefix_peak, new_peak)
    prefix_factor = jnp.exp(prefix_peak - peak)
    new_factor = jnp.exp(new_peak - peak)
    numerator = prefix_sum * prefix_factor[..., None] + new_sum * new_factor[..., None]
    denominator = prefix_total * prefix_factor + new_total * new_factor
    attended = (numerator / denominator[..., None]).astype(jnp.bfloat16).reshape(rows, cut)

    partial_heads = jnp.dot(attended, out_weight, preferred_element_type=jnp.float32)
    chunk = lax.dynamic_slice_in_dim(partial_heads, first_column, span, 1)
    chunk = chunk + local[:, cut + 2 * head :].astype(jnp.float32)
    partial_heads = lax.dynamic_update_slice_in_dim(partial_heads, chunk, first_column, 1)
    mine = rows // shares
    along_y = [[at * 2 + half for at in range(4)] for half in range(2)]
    arrived = lax.all_to_all(
        partial_heads, "vocab", 0, 0, tiled=True, axis_index_groups=along_y
    ).reshape(4, 2, mine, width)
    kept = jnp.sum(lax.dynamic_index_in_dim(arrived, z_hi, 1, False), axis=0)
    given = jnp.sum(lax.dynamic_index_in_dim(arrived, 1 - z_hi, 1, False), axis=0)
    hidden = kept + lax.ppermute(given, BOTH, HALVES)
    normed = rms_scale(hidden, final_gain).astype(jnp.bfloat16)

    rounds = ring_gather([normed[:, a:b] for a, b in PIECES])
    logits, other_logits, local_sum = head_logits(rounds, head_weight, other_weight, mine)
    crossed = swap_cores(other_logits)

    places = jnp.arange(4, dtype=jnp.int32)
    near = lambda at: jnp.where(core == 0, at - places, places - at) % 4
    mine_order = (
        near(z)[:, None, None] * 16 + near(y)[None, :, None] * 4 + near(x)[None, None, :]
    ).reshape(64)
    local_sum = jnp.take(local_sum.reshape(64, mine), mine_order, axis=0)
    sample_at = jnp.sum(
        jnp.where(
            slot[None, :] == jnp.arange(samples, dtype=jnp.int32)[:, None],
            jnp.arange(samples, dtype=jnp.int32)[None, :],
            0,
        ),
        axis=1,
    )
    sent = jnp.concatenate([local_sum.reshape(64 * mine), sample_at.astype(jnp.float32)])
    over_grp = spread(sent, "grp")
    order = over_grp[:, 64 * mine :].astype(jnp.int32).reshape(-1)
    over_grp = log_sum(over_grp[:, : 64 * mine].reshape(8, 2, 64 * mine), 0)
    total = log_sum(spread(over_grp, "vocab").reshape(shares, 2, 64 * mine), 0)
    total = total.reshape(2, 2, 2, 4, 4, mine).transpose(2, 4, 0, 3, 1, 5)
    shape = (4, 4, 4, mine, head_weight.shape[1])
    return ordered_output(
        order,
        jnp.stack([core, x, y, z]).astype(jnp.int32),
        logits.reshape(shape),
        crossed.reshape(shape),
        total.reshape(16, 8, mine, 1),
    )


def solution(mesh):
    placed = (
        P("grp", None, None),
        P(),
        P(None, "vocab"),
        P(None, "vocab"),
        P(None, "vocab"),
        P("vocab", None),
        P(),
        P(None, ("grp", "vocab")),
        P("grp", "vocab", None, None),
        P("grp", "vocab", None, None),
        P("grp"),
    )
    return jax.shard_map(
        on_device,
        mesh=mesh,
        in_specs=placed,
        out_specs=P(None, None, ("grp", "vocab")),
        check_vma=False,
    )
```

```python
import functools

import jax
import jax.numpy as jnp
from jax import lax
from jax.experimental import pallas as pl
from jax.experimental.pallas import tpu as pltpu
from jax.sharding import PartitionSpec as P

BOTH = ("grp", "vocab")
RING = 4
PIECES = ((0, 1792), (1792, 3584), (3584, 5120))
ORDERS = ("xyz", "yzx", "zxy")


def place_of(flat):
    grp, vocab = divmod(flat, 8)
    z_lo, rest = divmod(grp, 8)
    x, core = divmod(rest, 2)
    y, z_hi = divmod(vocab, 2)
    return {"x": x, "y": y, "z": z_hi * 2 + z_lo, "core": core}


def flat_of(at):
    grp = (at["z"] % 2) * 8 + at["x"] * 2 + at["core"]
    return grp * 8 + at["y"] * 2 + at["z"] // 2


def ring_pairs(axis):
    pairs = []
    for source in range(128):
        at = place_of(source)
        at[axis] = (at[axis] + (1 if at["core"] == 0 else -1)) % RING
        pairs.append((source, flat_of(at)))
    return pairs


def swap_pairs(axis, distance, size):
    pairs = []
    for source in range(128):
        at = place_of(source)
        at[axis] = (at[axis] + distance) % size
        pairs.append((source, flat_of(at)))
    return pairs


STEP = {axis: ring_pairs(axis) for axis in "xyz"}
CORES = swap_pairs("core", 1, 2)
HALVES = swap_pairs("z", 2, RING)


def swap_cores(block):
    return lax.ppermute(block, BOTH, CORES)


def ring_gather(blocks):
    held = list(blocks)
    for stage in range(3):
        rounds = [[part] for part in held]
        for _ in range(RING - 1):
            for k, order in enumerate(ORDERS):
                rounds[k].append(lax.ppermute(rounds[k][-1], BOTH, STEP[order[stage]]))
        if stage < 2:
            held = [jnp.stack(parts) for parts in rounds]
    return rounds


def weight_copies(k, own_w, other_w, weights, sems):
    a, b = PIECES[k]
    half = own_w.shape[1]
    rows = pl.ds(a, b - a)
    return [
        pltpu.make_async_copy(own_w.at[rows], weights[k].at[:, pl.ds(0, half)], sems.at[k, 0]),
        pltpu.make_async_copy(other_w.at[rows], weights[k].at[:, pl.ds(half, half)], sems.at[k, 1]),
    ]


def early_kernel(*refs):
    parts = (refs[0:3], refs[3:6], refs[6:9])
    own_w, other_w, out, *work = refs[9:]
    lhs, weights, (total, lhs_sem, w_sem, out_sem) = work[0:3], work[3:6], work[6:]
    mine, cols = out.shape[3:]

    def copies(k):
        return [
            pltpu.make_async_copy(parts[k][r], lhs[k].at[r], lhs_sem.at[k, r]) for r in range(3)
        ] + weight_copies(k, own_w, other_w, weights, w_sem)

    for k in range(3):
        for copy in copies(k):
            copy.start()

    for copy in copies(0):
        copy.wait()

    def first(z, carry):
        rows = lhs[0][z].reshape(16 * mine, -1)
        fresh = jnp.dot(rows, weights[0][...], preferred_element_type=jnp.float32)
        total[z] = fresh.reshape(4, 4, mine, cols)
        return carry

    lax.fori_loop(0, 3, first, 0)
    total[3] = jnp.zeros((4, 4, mine, cols), jnp.float32)
    for copy in copies(1):
        copy.wait()

    def second(z, carry):
        rows = jnp.concatenate([lhs[1][x, z, y] for y in range(4) for x in range(3)], axis=0)
        fresh = jnp.dot(rows, weights[1][...], preferred_element_type=jnp.float32)
        total[z, :, 0:3] += fresh.reshape(4, 3, mine, cols)
        return carry

    lax.fori_loop(0, 4, second, 0)
    for copy in copies(2):
        copy.wait()
    write = lambda z: pltpu.make_async_copy(total.at[z], out.at[z], out_sem.at[z])

    def third(z, carry):
        rows = jnp.concatenate([lhs[2][y, x, z] for y in range(3) for x in range(4)], axis=0)
        fresh = jnp.dot(rows, weights[2][...], preferred_element_type=jnp.float32)
        total[z, 0:3] += fresh.reshape(3, 4, mine, cols)
        write(z).start()
        return carry

    lax.fori_loop(0, 4, third, 0)
    for z in range(4):
        write(z).wait()


def late_kernel(
    last_a, last_b, last_c, own_w, other_w, early, own_out, other_out, sums, *work
):
    lhs, weights, (total, lhs_sem, w_sem, in_sem, out_sem) = work[0:3], work[3:6], work[6:]
    mine, cols = early.shape[3:]
    half = own_w.shape[1]
    parts = (last_a, last_b, last_c)
    load = pltpu.make_async_copy(early, total, in_sem)

    def copies(k):
        return [pltpu.make_async_copy(parts[k], lhs[k], lhs_sem.at[k])] + weight_copies(
            k, own_w, other_w, weights, w_sem
        )

    for copy in copies(0):
        copy.start()
    load.start()
    for k in (1, 2):
        for copy in copies(k):
            copy.start()

    def product(k):
        for copy in copies(k):
            copy.wait()
        rows = lhs[k][...].reshape(16 * mine, -1)
        fresh = jnp.dot(rows, weights[k][...], preferred_element_type=jnp.float32)
        return fresh.reshape(4, 4, mine, cols)

    fresh = product(0)
    load.wait()
    total[3] += fresh
    total[:, :, 3] += product(1)
    fresh = product(2)
    for x in range(4):
        for z in range(4):
            total[z, 3, x] += fresh[x, z]

    def out_copies(z):
        return [
            pltpu.make_async_copy(
                total.at[z, :, :, :, pl.ds(0, half)], own_out.at[z], out_sem.at[z, 0]
            ),
            pltpu.make_async_copy(
                total.at[z, :, :, :, pl.ds(half, half)], other_out.at[z], out_sem.at[z, 1]
            ),
        ]

    def finish(z, carry):
        for copy in out_copies(z):
            copy.start()
        rows = total[z].reshape(16 * mine, cols)
        top = jnp.max(rows, axis=1, keepdims=True)
        mass = jnp.sum(jnp.exp(rows - top), axis=1, keepdims=True)
        at = pl.ds(pl.multiple_of(z * 16 * mine, 16 * mine), 16 * mine)
        sums[at] = top + jnp.log(mass)
        return carry

    lax.fori_loop(0, 4, finish, 0)
    for z in range(4):
        for copy in out_copies(z):
            copy.wait()


def head_logits(rounds, own_w, other_w, mine):
    half = own_w.shape[1]
    rows = 64 * mine
    anywhere = pl.BlockSpec(memory_space=pl.ANY)
    widths = [b - a for a, b in PIECES]
    shape = (4, 4, 4, mine)
    weight_room = [pltpu.VMEM((w, 2 * half), jnp.bfloat16) for w in widths]
    params = pltpu.CompilerParams(vmem_limit_bytes=48 * 2**20)
    flops = 2 * rows * 5120 * 2 * half
    early = pl.pallas_call(
        early_kernel,
        out_shape=jax.ShapeDtypeStruct(shape + (2 * half,), jnp.float32),
        in_specs=[anywhere] * 11,
        out_specs=anywhere,
        scratch_shapes=[pltpu.VMEM((3, 4, 4, mine, w), jnp.bfloat16) for w in widths]
        + weight_room
        + [
            pltpu.VMEM(shape + (2 * half,), jnp.float32),
            pltpu.SemaphoreType.DMA((3, 3)),
            pltpu.SemaphoreType.DMA((3, 2)),
            pltpu.SemaphoreType.DMA((4,)),
        ],
        compiler_params=params,
        cost_estimate=pl.CostEstimate(
            flops=flops * 3 // 4, bytes_accessed=26 * 10**6, transcendentals=0
        ),
        name="head_early",
    )(*[block for piece in rounds for block in piece[:3]], own_w, other_w)
    return pl.pallas_call(
        late_kernel,
        out_shape=(
            jax.ShapeDtypeStruct(shape + (half,), jnp.float32),
            jax.ShapeDtypeStruct(shape + (half,), jnp.float32),
            jax.ShapeDtypeStruct((rows, 1), jnp.float32),
        ),
        in_specs=[anywhere] * 6,
        out_specs=(anywhere, anywhere, pl.BlockSpec(memory_space=pltpu.VMEM)),
        scratch_shapes=[pltpu.VMEM((4, 4, mine, w), jnp.bfloat16) for w in widths]
        + weight_room
        + [
            pltpu.VMEM(shape + (2 * half,), jnp.float32),
            pltpu.SemaphoreType.DMA((3,)),
            pltpu.SemaphoreType.DMA((3, 2)),
            pltpu.SemaphoreType.DMA,
            pltpu.SemaphoreType.DMA((4, 2)),
        ],
        compiler_params=params,
        cost_estimate=pl.CostEstimate(
            flops=flops // 4, bytes_accessed=26 * 10**6, transcendentals=rows * 2 * half
        ),
        name="head_late",
    )(*[piece[3] for piece in rounds], own_w, other_w, early)


def front_kernel(
    prompts, column, embedded, gain, query_w, key_w, value_w, out, order, seen, raw, weights, sems
):
    samples, steps, width = embedded.shape
    cuts = (0, query_w.shape[1], query_w.shape[1] + key_w.shape[1])
    copies = [
        pltpu.make_async_copy(w, weights.at[:, pl.ds(at, w.shape[1])], sems.at[i])
        for i, (w, at) in enumerate(zip((query_w, key_w, value_w), cuts))
    ]
    for copy in copies:
        copy.start()
    for p in range(samples // 2):
        seen[p] = 0
    for i in range(samples):
        p = prompts[i]
        slot = p * 2 + seen[p]
        seen[p] = seen[p] + 1
        order[slot] = i
    for slot in range(samples):
        raw[slot * steps : (slot + 1) * steps] = embedded[order[slot]].astype(jnp.float32)
    rows = raw[...]
    mean_sq = jnp.mean(rows * rows, axis=-1, keepdims=True)
    normed = (rows * lax.rsqrt(mean_sq + 1e-06) * gain[...]).astype(jnp.bfloat16)
    span = out.shape[1] - weights.shape[1]
    at = pl.multiple_of(column[0], 128)
    out[:, weights.shape[1] :] = raw[:, pl.ds(at, span)].astype(jnp.bfloat16)
    for copy in copies:
        copy.wait()
    out[:, : weights.shape[1]] = jnp.dot(
        normed, weights[...], preferred_element_type=jnp.float32
    ).astype(jnp.bfloat16)


def front(sample_prompt, column, embedded, gain, query_w, key_w, value_w, span):
    samples, steps, width = embedded.shape
    anywhere = pl.BlockSpec(memory_space=pl.ANY)
    scalars = pl.BlockSpec(memory_space=pltpu.SMEM)
    vector = pl.BlockSpec(memory_space=pltpu.VMEM)
    cols = query_w.shape[1] + key_w.shape[1] + value_w.shape[1]
    return pl.pallas_call(
        front_kernel,
        out_shape=(
            jax.ShapeDtypeStruct((samples * steps, cols + span), jnp.bfloat16),
            jax.ShapeDtypeStruct((samples,), jnp.int32),
        ),
        in_specs=[scalars, scalars, vector, vector, anywhere, anywhere, anywhere],
        out_specs=(vector, scalars),
        scratch_shapes=[
            pltpu.SMEM((samples // 2,), jnp.int32),
            pltpu.VMEM((samples * steps, width), jnp.float32),
            pltpu.VMEM((width, cols), jnp.bfloat16),
            pltpu.SemaphoreType.DMA((3,)),
        ],
        compiler_params=pltpu.CompilerParams(vmem_limit_bytes=40 * 2**20),
        cost_estimate=pl.CostEstimate(
            flops=2 * samples * steps * width * cols, bytes_accessed=10**7, transcendentals=0
        ),
        name="front",
    )(sample_prompt, column, embedded, gain.reshape(1, -1), query_w, key_w, value_w)


def attend_kernel(steps, local, keys, values, out):
    head = keys.shape[1]
    rows = local.shape[0]
    groups = out.shape[1] // head
    scale = 1.0 / head**0.5
    new_keys = local[:, groups * head : (groups + 1) * head]
    new_values = local[:, (groups + 1) * head : (groups + 2) * head]
    at_row = lax.broadcasted_iota(jnp.int32, (rows, rows), 0)
    at_col = lax.broadcasted_iota(jnp.int32, (rows, rows), 1)
    seen = (at_row // steps == at_col // steps) & (at_col <= at_row)
    across = (((1,), (1,)), ((), ()))

    def parts(scores, value_rows):
        peak = jnp.max(scores, axis=1, keepdims=True)
        powers = jnp.exp(scores - peak)
        weighted = jnp.dot(
            powers.astype(jnp.bfloat16), value_rows, preferred_element_type=jnp.float32
        )
        return peak, jnp.sum(powers, axis=1, keepdims=True), weighted

    for g in range(groups):
        span = slice(g * head, (g + 1) * head)
        queries = local[:, span]
        scores = lax.dot_general(queries, keys[...], across, preferred_element_type=jnp.float32)
        prefix_peak, prefix_total, prefix_sum = parts(scores * scale, values[...])
        scores = lax.dot_general(queries, new_keys, across, preferred_element_type=jnp.float32)
        new_peak, new_total, new_sum = parts(jnp.where(seen, scores * scale, -1e30), new_values)
        peak = jnp.maximum(prefix_peak, new_peak)
        prefix_factor = jnp.exp(prefix_peak - peak)
        new_factor = jnp.exp(new_peak - peak)
        total = prefix_total * prefix_factor + new_total * new_factor
        attended = (prefix_sum * prefix_factor + new_sum * new_factor) / total
        out[:, span] = attended.astype(jnp.bfloat16)


def attend(local, keys, values, steps, cols):
    vector = pl.BlockSpec(memory_space=pltpu.VMEM)
    return pl.pallas_call(
        functools.partial(attend_kernel, steps),
        out_shape=jax.ShapeDtypeStruct((local.shape[0], cols), jnp.bfloat16),
        in_specs=[vector] * 3,
        out_specs=vector,
        compiler_params=pltpu.CompilerParams(vmem_limit_bytes=40 * 2**20),
        name="attend",
    )(local, keys, values)


def output_kernel(order, place, own, other, totals, out):
    pair = pl.program_id(0)
    y, z_hi = pair // 2, pair % 2
    core, x_here, y_here, z_here = place[0], place[1], place[2], place[3]
    for ref, plane in ((own, core), (other, 1 - core)):
        sign = 1 - 2 * plane
        away = lambda here, there: (sign * (here - there)) & 3
        for z_lo in range(2):
            for x in range(4):
                prompt = z_lo * 8 + x * 2 + plane
                block = ref[away(z_here, z_hi * 2 + z_lo), away(y_here, y), away(x_here, x)]
                block = block - totals[prompt, pair]
                for row in range(4):
                    near, which = divmod(row, 2)
                    to = order[(pair * 2 + near) * 32 + prompt * 2 + which]
                    out[near * 32 + to] = block[row * 4 : row * 4 + 4]


def ordered_output(order, place, own, other, totals):
    width = own.shape[-1]
    whole = lambda a: pl.BlockSpec(a.shape, lambda i, *_: (0,) * a.ndim)
    return pl.pallas_call(
        output_kernel,
        out_shape=jax.ShapeDtypeStruct((512, 4, width), jnp.float32),
        grid_spec=pltpu.PrefetchScalarGridSpec(
            num_scalar_prefetch=2,
            grid=(8,),
            in_specs=[whole(own), whole(other), whole(totals)],
            out_specs=pl.BlockSpec((64, 4, width), lambda i, *_: (i, 0, 0)),
        ),
        compiler_params=pltpu.CompilerParams(vmem_limit_bytes=52 * 2**20),
        name="output",
    )(order, place, own, other, totals)


def rms_scale(rows, gain):
    mean_sq = jnp.mean(rows * rows, axis=-1, keepdims=True)
    return rows * lax.rsqrt(mean_sq + 1e-06) * gain


def log_sum(values, axis):
    top = jnp.max(values, axis=axis, keepdims=True)
    return jnp.squeeze(top, axis) + jnp.log(jnp.sum(jnp.exp(values - top), axis=axis))


def spread(values, axis):
    copies = lax.axis_size(axis)
    return lax.all_to_all(
        jnp.broadcast_to(values[None], (copies,) + values.shape), axis, 0, 0, tiled=True
    )


def on_device(
    embedded,
    attn_gain,
    query_weight,
    key_weight,
    value_weight,
    out_weight,
    final_gain,
    head_weight,
    prefix_keys,
    prefix_values,
    sample_prompt,
):
    samples, steps, width = embedded.shape
    rows = samples * steps
    cols = query_weight.shape[1]
    core = lax.axis_index("grp") % 2
    z_hi = lax.axis_index("vocab") % 2
    z = z_hi * 2 + lax.axis_index("grp") // 8
    y = lax.axis_index("vocab") // 2
    x = (lax.axis_index("grp") // 2) % 4
    shares = lax.axis_size("vocab")
    mine = rows // shares
    span = width // shares
    half = width // 2
    other_weight = swap_cores(head_weight)

    part = cols // 2
    leaving = lax.dynamic_slice(out_weight, (core * part, (1 - z_hi) * half), (part, half))
    far_same = lax.ppermute(leaving, BOTH, HALVES)
    far_other = swap_cores(far_same)

    own_columns = z_hi * half + y * span
    sorted_rows, sample_at = front(
        sample_prompt,
        own_columns.reshape(1).astype(jnp.int32),
        embedded,
        attn_gain,
        query_weight,
        key_weight,
        value_weight,
        span,
    )
    local = lax.all_to_all(sorted_rows, "grp", 0, 0, tiled=True)

    attended = attend(local, prefix_keys[0, 0], prefix_values[0, 0], steps, cols)
    far = lax.ppermute(attended, BOTH, HALVES)

    def product(a, w):
        return jnp.dot(a, w, preferred_element_type=jnp.float32)

    partial_heads = (
        product(attended, lax.dynamic_slice_in_dim(out_weight, z_hi * half, half, 1))
        + product(lax.dynamic_slice_in_dim(far, core * part, part, 1), far_same)
        + product(lax.dynamic_slice_in_dim(far, (1 - core) * part, part, 1), far_other)
    )
    chunk = lax.dynamic_slice_in_dim(partial_heads, y * span, span, 1)
    chunk = chunk + local[:, -span:].astype(jnp.float32)
    partial_heads = lax.dynamic_update_slice_in_dim(partial_heads, chunk, y * span, 1)
    along_y = [[at * 2 + half_at for at in range(4)] for half_at in range(2)]
    arrived = lax.all_to_all(
        partial_heads, "vocab", 0, 0, tiled=True, axis_index_groups=along_y
    ).reshape(4, 2, mine, half)
    kept = jnp.sum(lax.dynamic_index_in_dim(arrived, z_hi, 1, False), axis=0)
    given = jnp.sum(lax.dynamic_index_in_dim(arrived, 1 - z_hi, 1, False), axis=0)
    taken = lax.ppermute(given, BOTH, HALVES)
    hidden = jnp.where(
        z_hi == 0,
        jnp.concatenate([kept, taken], axis=1),
        jnp.concatenate([taken, kept], axis=1),
    )
    normed = rms_scale(hidden, final_gain).astype(jnp.bfloat16)

    rounds = ring_gather([normed[:, a:b] for a, b in PIECES])
    logits, other_logits, local_sum = head_logits(rounds, head_weight, other_weight, mine)
    crossed = swap_cores(other_logits)

    places = jnp.arange(4, dtype=jnp.int32)
    near = lambda at: jnp.where(core == 0, at - places, places - at) % 4
    mine_order = (
        near(z)[:, None, None] * 16 + near(y)[None, :, None] * 4 + near(x)[None, None, :]
    ).reshape(64)
    local_sum = jnp.take(local_sum.reshape(64, mine), mine_order, axis=0)
    sent = jnp.concatenate([local_sum.reshape(64 * mine), sample_at.astype(jnp.float32)])
    over_grp = spread(sent, "grp")
    order = over_grp[:, 64 * mine :].astype(jnp.int32).reshape(-1)
    over_grp = log_sum(over_grp[:, : 64 * mine].reshape(8, 2, 64 * mine), 0)
    total = log_sum(spread(over_grp, "vocab").reshape(shares, 2, 64 * mine), 0)
    total = total.reshape(2, 2, 2, 4, 4, mine).transpose(2, 4, 0, 3, 1, 5)
    return ordered_output(
        order,
        jnp.stack([core, x, y, z]).astype(jnp.int32),
        logits,
        crossed,
        total.reshape(16, 8, mine, 1),
    )


def solution(mesh):
    placed = (
        P("grp", None, None),
        P(),
        P(None, "vocab"),
        P(None, "vocab"),
        P(None, "vocab"),
        P("vocab", None),
        P(),
        P(None, ("grp", "vocab")),
        P("grp", "vocab", None, None),
        P("grp", "vocab", None, None),
        P("grp"),
    )
    return jax.shard_map(
        on_device,
        mesh=mesh,
        in_specs=placed,
        out_specs=P(None, None, ("grp", "vocab")),
        check_vma=False,
    )
```

```python
import functools

import jax
import jax.numpy as jnp
from jax import lax
from jax.experimental import pallas as pl
from jax.experimental.pallas import tpu as pltpu
from jax.sharding import PartitionSpec as P

BOTH = ("grp", "vocab")
RING = 4
PIECES = ((0, 1792), (1792, 3584), (3584, 5120))
ORDERS = ("xyz", "yzx", "zxy")


def place_of(flat):
    grp, vocab = divmod(flat, 8)
    z_lo, rest = divmod(grp, 8)
    x, core = divmod(rest, 2)
    y, z_hi = divmod(vocab, 2)
    return {"x": x, "y": y, "z": z_hi * 2 + z_lo, "core": core}


def flat_of(at):
    grp = (at["z"] % 2) * 8 + at["x"] * 2 + at["core"]
    return grp * 8 + at["y"] * 2 + at["z"] // 2


def ring_pairs(axis):
    pairs = []
    for source in range(128):
        at = place_of(source)
        at[axis] = (at[axis] + (1 if at["core"] == 0 else -1)) % RING
        pairs.append((source, flat_of(at)))
    return pairs


def swap_pairs(axis, distance, size):
    pairs = []
    for source in range(128):
        at = place_of(source)
        at[axis] = (at[axis] + distance) % size
        pairs.append((source, flat_of(at)))
    return pairs


STEP = {axis: ring_pairs(axis) for axis in "xyz"}
CORES = swap_pairs("core", 1, 2)
HALVES = swap_pairs("z", 2, RING)


def swap_cores(block):
    return lax.ppermute(block, BOTH, CORES)


def ring_gather(blocks):
    held = list(blocks)
    for stage in range(3):
        rounds = [[part] for part in held]
        for step in range(RING - 1):
            if stage > 0 and step == 0 or stage == 2 and step == RING - 2:
                tips = lax.optimization_barrier(tuple(parts[-1] for parts in rounds))
                rounds = [parts[:-1] + [tip] for parts, tip in zip(rounds, tips)]
            for k, order in enumerate(ORDERS):
                rounds[k].append(lax.ppermute(rounds[k][-1], BOTH, STEP[order[stage]]))
        if stage < 2:
            held = [jnp.stack(parts) for parts in rounds]
    return rounds


def weight_copies(k, own_w, other_w, weights, sems):
    a, b = PIECES[k]
    half = own_w.shape[1]
    rows = pl.ds(a, b - a)
    return [
        pltpu.make_async_copy(own_w.at[rows], weights[k].at[:, pl.ds(0, half)], sems.at[k, 0]),
        pltpu.make_async_copy(other_w.at[rows], weights[k].at[:, pl.ds(half, half)], sems.at[k, 1]),
    ]


def early_kernel(*refs):
    parts = (refs[0:3], refs[3:6], refs[6:9])
    own_w, other_w, out, *work = refs[9:]
    lhs, weights, (total, lhs_sem, w_sem, out_sem) = work[0:3], work[3:6], work[6:]
    mine, cols = out.shape[3:]

    def copies(k):
        return [
            pltpu.make_async_copy(parts[k][r], lhs[k].at[r], lhs_sem.at[k, r]) for r in range(3)
        ] + weight_copies(k, own_w, other_w, weights, w_sem)

    for k in range(3):
        for copy in copies(k):
            copy.start()

    for copy in copies(0):
        copy.wait()

    def first(z, carry):
        rows = lhs[0][z].reshape(16 * mine, -1)
        fresh = jnp.dot(rows, weights[0][...], preferred_element_type=jnp.float32)
        total[z] = fresh.reshape(4, 4, mine, cols)
        return carry

    lax.fori_loop(0, 3, first, 0)
    total[3] = jnp.zeros((4, 4, mine, cols), jnp.float32)
    for copy in copies(1):
        copy.wait()

    def second(z, carry):
        rows = jnp.concatenate([lhs[1][x, z, y] for y in range(4) for x in range(3)], axis=0)
        fresh = jnp.dot(rows, weights[1][...], preferred_element_type=jnp.float32)
        total[z, :, 0:3] += fresh.reshape(4, 3, mine, cols)
        return carry

    lax.fori_loop(0, 4, second, 0)
    for copy in copies(2):
        copy.wait()
    write = lambda z: pltpu.make_async_copy(total.at[z], out.at[z], out_sem.at[z])

    def third(z, carry):
        rows = jnp.concatenate([lhs[2][y, x, z] for y in range(3) for x in range(4)], axis=0)
        fresh = jnp.dot(rows, weights[2][...], preferred_element_type=jnp.float32)
        total[z, 0:3] += fresh.reshape(3, 4, mine, cols)
        write(z).start()
        return carry

    lax.fori_loop(0, 4, third, 0)
    for z in range(4):
        write(z).wait()


def late_kernel(
    last_a, last_b, last_c, own_w, other_w, early, own_out, other_out, sums, *work
):
    lhs, weights, (total, lhs_sem, w_sem, in_sem, out_sem) = work[0:3], work[3:6], work[6:]
    mine, cols = early.shape[3:]
    half = own_w.shape[1]
    parts = (last_a, last_b, last_c)
    load = pltpu.make_async_copy(early, total, in_sem)

    def copies(k):
        return [pltpu.make_async_copy(parts[k], lhs[k], lhs_sem.at[k])] + weight_copies(
            k, own_w, other_w, weights, w_sem
        )

    for copy in copies(0):
        copy.start()
    load.start()
    for k in (1, 2):
        for copy in copies(k):
            copy.start()

    def product(k):
        for copy in copies(k):
            copy.wait()
        rows = lhs[k][...].reshape(16 * mine, -1)
        fresh = jnp.dot(rows, weights[k][...], preferred_element_type=jnp.float32)
        return fresh.reshape(4, 4, mine, cols)

    fresh = product(0)
    load.wait()
    total[3] += fresh
    total[:, :, 3] += product(1)
    fresh = product(2)
    for x in range(4):
        for z in range(4):
            total[z, 3, x] += fresh[x, z]

    def out_copies(z):
        return [
            pltpu.make_async_copy(
                total.at[z, :, :, :, pl.ds(0, half)], own_out.at[z], out_sem.at[z, 0]
            ),
            pltpu.make_async_copy(
                total.at[z, :, :, :, pl.ds(half, half)], other_out.at[z], out_sem.at[z, 1]
            ),
        ]

    def finish(z, carry):
        for copy in out_copies(z):
            copy.start()
        rows = total[z].reshape(16 * mine, cols)
        top = jnp.max(rows, axis=1, keepdims=True)
        mass = jnp.sum(jnp.exp(rows - top), axis=1, keepdims=True)
        at = pl.ds(pl.multiple_of(z * 16 * mine, 16 * mine), 16 * mine)
        sums[at] = top + jnp.log(mass)
        return carry

    lax.fori_loop(0, 4, finish, 0)
    for z in range(4):
        for copy in out_copies(z):
            copy.wait()


def head_logits(rounds, own_w, other_w, mine):
    half = own_w.shape[1]
    rows = 64 * mine
    anywhere = pl.BlockSpec(memory_space=pl.ANY)
    widths = [b - a for a, b in PIECES]
    shape = (4, 4, 4, mine)
    weight_room = [pltpu.VMEM((w, 2 * half), jnp.bfloat16) for w in widths]
    params = pltpu.CompilerParams(vmem_limit_bytes=48 * 2**20)
    flops = 2 * rows * 5120 * 2 * half
    early = pl.pallas_call(
        early_kernel,
        out_shape=jax.ShapeDtypeStruct(shape + (2 * half,), jnp.float32),
        in_specs=[anywhere] * 11,
        out_specs=anywhere,
        scratch_shapes=[pltpu.VMEM((3, 4, 4, mine, w), jnp.bfloat16) for w in widths]
        + weight_room
        + [
            pltpu.VMEM(shape + (2 * half,), jnp.float32),
            pltpu.SemaphoreType.DMA((3, 3)),
            pltpu.SemaphoreType.DMA((3, 2)),
            pltpu.SemaphoreType.DMA((4,)),
        ],
        compiler_params=params,
        cost_estimate=pl.CostEstimate(
            flops=flops * 3 // 4, bytes_accessed=26 * 10**6, transcendentals=0
        ),
        name="head_early",
    )(*[block for piece in rounds for block in piece[:3]], own_w, other_w)
    return pl.pallas_call(
        late_kernel,
        out_shape=(
            jax.ShapeDtypeStruct(shape + (half,), jnp.float32),
            jax.ShapeDtypeStruct(shape + (half,), jnp.float32),
            jax.ShapeDtypeStruct((rows, 1), jnp.float32),
        ),
        in_specs=[anywhere] * 6,
        out_specs=(anywhere, anywhere, pl.BlockSpec(memory_space=pltpu.VMEM)),
        scratch_shapes=[pltpu.VMEM((4, 4, mine, w), jnp.bfloat16) for w in widths]
        + weight_room
        + [
            pltpu.VMEM(shape + (2 * half,), jnp.float32),
            pltpu.SemaphoreType.DMA((3,)),
            pltpu.SemaphoreType.DMA((3, 2)),
            pltpu.SemaphoreType.DMA,
            pltpu.SemaphoreType.DMA((4, 2)),
        ],
        compiler_params=params,
        cost_estimate=pl.CostEstimate(
            flops=flops // 4, bytes_accessed=26 * 10**6, transcendentals=rows * 2 * half
        ),
        name="head_late",
    )(*[piece[3] for piece in rounds], own_w, other_w, early)


def front_kernel(
    prompts, column, embedded, gain, query_w, key_w, value_w, out, order, seen, raw, weights, sems
):
    samples, steps, width = embedded.shape
    cuts = (0, query_w.shape[1], query_w.shape[1] + key_w.shape[1])
    copies = [
        pltpu.make_async_copy(w, weights.at[:, pl.ds(at, w.shape[1])], sems.at[i])
        for i, (w, at) in enumerate(zip((query_w, key_w, value_w), cuts))
    ]
    for copy in copies:
        copy.start()
    for p in range(samples // 2):
        seen[p] = 0
    for i in range(samples):
        p = prompts[i]
        slot = p * 2 + seen[p]
        seen[p] = seen[p] + 1
        order[slot] = i
    for slot in range(samples):
        raw[slot * steps : (slot + 1) * steps] = embedded[order[slot]].astype(jnp.float32)
    rows = raw[...]
    mean_sq = jnp.mean(rows * rows, axis=-1, keepdims=True)
    normed = (rows * lax.rsqrt(mean_sq + 1e-06) * gain[...]).astype(jnp.bfloat16)
    span = out.shape[1] - weights.shape[1]
    at = pl.multiple_of(column[0], 128)
    out[:, weights.shape[1] :] = raw[:, pl.ds(at, span)].astype(jnp.bfloat16)
    for copy in copies:
        copy.wait()
    out[:, : weights.shape[1]] = jnp.dot(
        normed, weights[...], preferred_element_type=jnp.float32
    ).astype(jnp.bfloat16)


def front(sample_prompt, column, embedded, gain, query_w, key_w, value_w, span):
    samples, steps, width = embedded.shape
    anywhere = pl.BlockSpec(memory_space=pl.ANY)
    scalars = pl.BlockSpec(memory_space=pltpu.SMEM)
    vector = pl.BlockSpec(memory_space=pltpu.VMEM)
    cols = query_w.shape[1] + key_w.shape[1] + value_w.shape[1]
    return pl.pallas_call(
        front_kernel,
        out_shape=(
            jax.ShapeDtypeStruct((samples * steps, cols + span), jnp.bfloat16),
            jax.ShapeDtypeStruct((samples,), jnp.int32),
        ),
        in_specs=[scalars, scalars, vector, vector, anywhere, anywhere, anywhere],
        out_specs=(vector, scalars),
        scratch_shapes=[
            pltpu.SMEM((samples // 2,), jnp.int32),
            pltpu.VMEM((samples * steps, width), jnp.float32),
            pltpu.VMEM((width, cols), jnp.bfloat16),
            pltpu.SemaphoreType.DMA((3,)),
        ],
        compiler_params=pltpu.CompilerParams(vmem_limit_bytes=60 * 2**20),
        cost_estimate=pl.CostEstimate(
            flops=2 * samples * steps * width * cols, bytes_accessed=10**7, transcendentals=0
        ),
        name="front",
    )(sample_prompt, column, embedded, gain.reshape(1, -1), query_w, key_w, value_w)


def attend_kernel(steps, local, keys, values, out):
    head = keys.shape[1]
    rows = local.shape[0]
    groups = out.shape[1] // head
    scale = 1.0 / head**0.5
    new_keys = local[:, groups * head : (groups + 1) * head]
    new_values = local[:, (groups + 1) * head : (groups + 2) * head]
    at_row = lax.broadcasted_iota(jnp.int32, (rows, rows), 0)
    at_col = lax.broadcasted_iota(jnp.int32, (rows, rows), 1)
    seen = (at_row // steps == at_col // steps) & (at_col <= at_row)
    across = (((1,), (1,)), ((), ()))

    def parts(scores, value_rows):
        peak = jnp.max(scores, axis=1, keepdims=True)
        powers = jnp.exp(scores - peak)
        weighted = jnp.dot(
            powers.astype(jnp.bfloat16), value_rows, preferred_element_type=jnp.float32
        )
        return peak, jnp.sum(powers, axis=1, keepdims=True), weighted

    for g in range(groups):
        span = slice(g * head, (g + 1) * head)
        queries = local[:, span]
        scores = lax.dot_general(queries, keys[...], across, preferred_element_type=jnp.float32)
        prefix_peak, prefix_total, prefix_sum = parts(scores * scale, values[...])
        scores = lax.dot_general(queries, new_keys, across, preferred_element_type=jnp.float32)
        new_peak, new_total, new_sum = parts(jnp.where(seen, scores * scale, -1e30), new_values)
        peak = jnp.maximum(prefix_peak, new_peak)
        prefix_factor = jnp.exp(prefix_peak - peak)
        new_factor = jnp.exp(new_peak - peak)
        total = prefix_total * prefix_factor + new_total * new_factor
        attended = (prefix_sum * prefix_factor + new_sum * new_factor) / total
        out[:, span] = attended.astype(jnp.bfloat16)


def attend(local, keys, values, steps, cols):
    vector = pl.BlockSpec(memory_space=pltpu.VMEM)
    return pl.pallas_call(
        functools.partial(attend_kernel, steps),
        out_shape=jax.ShapeDtypeStruct((local.shape[0], cols), jnp.bfloat16),
        in_specs=[vector] * 3,
        out_specs=vector,
        compiler_params=pltpu.CompilerParams(vmem_limit_bytes=40 * 2**20),
        name="attend",
    )(local, keys, values)


def output_kernel(order, place, own, other, totals, out):
    pair = pl.program_id(0)
    y, z_hi = pair // 2, pair % 2
    core, x_here, y_here, z_here = place[0], place[1], place[2], place[3]
    for ref, plane in ((own, core), (other, 1 - core)):
        sign = 1 - 2 * plane
        away = lambda here, there: (sign * (here - there)) & 3
        for z_lo in range(2):
            for x in range(4):
                prompt = z_lo * 8 + x * 2 + plane
                block = ref[away(z_here, z_hi * 2 + z_lo), away(y_here, y), away(x_here, x)]
                block = block - totals[prompt, pair]
                for row in range(4):
                    near, which = divmod(row, 2)
                    to = order[(pair * 2 + near) * 32 + prompt * 2 + which]
                    out[near * 32 + to] = block[row * 4 : row * 4 + 4]


def ordered_output(order, place, own, other, totals):
    width = own.shape[-1]
    whole = lambda a: pl.BlockSpec(a.shape, lambda i, *_: (0,) * a.ndim)
    return pl.pallas_call(
        output_kernel,
        out_shape=jax.ShapeDtypeStruct((512, 4, width), jnp.float32),
        grid_spec=pltpu.PrefetchScalarGridSpec(
            num_scalar_prefetch=2,
            grid=(8,),
            in_specs=[whole(own), whole(other), whole(totals)],
            out_specs=pl.BlockSpec((64, 4, width), lambda i, *_: (i, 0, 0)),
        ),
        compiler_params=pltpu.CompilerParams(vmem_limit_bytes=52 * 2**20),
        name="output",
    )(order, place, own, other, totals)


def rms_scale(rows, gain):
    mean_sq = jnp.mean(rows * rows, axis=-1, keepdims=True)
    return rows * lax.rsqrt(mean_sq + 1e-06) * gain


def log_sum(values, axis):
    top = jnp.max(values, axis=axis, keepdims=True)
    return jnp.squeeze(top, axis) + jnp.log(jnp.sum(jnp.exp(values - top), axis=axis))


def spread(values, axis):
    copies = lax.axis_size(axis)
    return lax.all_to_all(
        jnp.broadcast_to(values[None], (copies,) + values.shape), axis, 0, 0, tiled=True
    )


def on_device(
    embedded,
    attn_gain,
    query_weight,
    key_weight,
    value_weight,
    out_weight,
    final_gain,
    head_weight,
    prefix_keys,
    prefix_values,
    sample_prompt,
):
    samples, steps, width = embedded.shape
    rows = samples * steps
    cols = query_weight.shape[1]
    core = lax.axis_index("grp") % 2
    z_hi = lax.axis_index("vocab") % 2
    z = z_hi * 2 + lax.axis_index("grp") // 8
    y = lax.axis_index("vocab") // 2
    x = (lax.axis_index("grp") // 2) % 4
    shares = lax.axis_size("vocab")
    mine = rows // shares
    span = width // shares
    half = width // 2
    other_weight = swap_cores(head_weight)

    own_columns = lax.axis_index("vocab") * span
    sorted_rows, sample_at = front(
        sample_prompt,
        own_columns.reshape(1).astype(jnp.int32),
        embedded,
        attn_gain,
        query_weight,
        key_weight,
        value_weight,
        span,
    )
    local = lax.all_to_all(sorted_rows, "grp", 0, 0, tiled=True)

    attended = attend(local, prefix_keys[0, 0], prefix_values[0, 0], steps, cols)
    attended, other_weight = lax.optimization_barrier((attended, other_weight))
    own_embedded = local[:, -span:].astype(jnp.float32)

    def product(part, attended):
        w = lax.slice_in_dim(out_weight, part * half, (part + 1) * half, axis=1)
        full = jnp.dot(attended, w, preferred_element_type=jnp.float32)
        at = (y * 2 + z_hi) % 4 * span
        chunk = lax.dynamic_slice_in_dim(full, at, span, 1)
        chunk = jnp.where((y * 2 + z_hi) // 4 == part, chunk + own_embedded, chunk)
        return lax.dynamic_update_slice_in_dim(full, chunk, at, 1)

    along_y = [[at * 2 + z_at for at in range(4)] for z_at in range(2)]

    def over_y(block):
        return lax.all_to_all(block, "vocab", 0, 0, tiled=True, axis_index_groups=along_y)

    def over_z(block, axis):
        kept = lax.dynamic_index_in_dim(block, z_hi, axis, False)
        given = lax.dynamic_index_in_dim(block, 1 - z_hi, axis, False)
        return kept, lax.ppermute(given, BOTH, HALVES)

    second, attended = lax.optimization_barrier((product(1, attended), attended))
    kept, taken = over_z(second.reshape(4, 2, mine, half), 1)
    first_y = jnp.sum(over_y(product(0, attended)).reshape(4, 2, mine, half), axis=0)
    second_z = kept + taken
    kept, taken = over_z(first_y, 0)
    second_y = jnp.sum(over_y(second_z.reshape(4 * mine, half)).reshape(4, mine, half), axis=0)
    hidden = jnp.concatenate([kept + taken, second_y], axis=1)
    normed = rms_scale(hidden, final_gain).astype(jnp.bfloat16)

    rounds = ring_gather([normed[:, a:b] for a, b in PIECES])
    logits, other_logits, local_sum = head_logits(rounds, head_weight, other_weight, mine)
    crossed = swap_cores(other_logits)

    places = jnp.arange(4, dtype=jnp.int32)
    near = lambda at: jnp.where(core == 0, at - places, places - at) % 4
    mine_order = (
        near(z)[:, None, None] * 16 + near(y)[None, :, None] * 4 + near(x)[None, None, :]
    ).reshape(64)
    local_sum = jnp.take(local_sum.reshape(64, mine), mine_order, axis=0)
    over_vocab = log_sum(spread(local_sum.reshape(64 * mine), "vocab"), 0)
    sent = jnp.concatenate([over_vocab, sample_at.astype(jnp.float32)])
    over_grp = spread(sent, "grp")
    order = over_grp[:, 64 * mine :].astype(jnp.int32).reshape(-1)
    total = log_sum(over_grp[:, : 64 * mine].reshape(8, 2, 64 * mine), 0)
    total = total.reshape(2, 2, 2, 4, 4, mine).transpose(2, 4, 0, 3, 1, 5)
    return ordered_output(
        order,
        jnp.stack([core, x, y, z]).astype(jnp.int32),
        logits,
        crossed,
        total.reshape(16, 8, mine, 1),
    )


def solution(mesh):
    placed = (
        P("grp", None, None),
        P(),
        P(None, "vocab"),
        P(None, "vocab"),
        P(None, "vocab"),
        P("vocab", None),
        P(),
        P(None, ("grp", "vocab")),
        P("grp", "vocab", None, None),
        P("grp", "vocab", None, None),
        P("grp"),
    )
    return jax.shard_map(
        on_device,
        mesh=mesh,
        in_specs=placed,
        out_specs=P(None, None, ("grp", "vocab")),
        check_vma=False,
    )
```

```python
import functools

import jax
import jax.numpy as jnp
from jax import lax
from jax.experimental import pallas as pl
from jax.experimental.pallas import tpu as pltpu
from jax.sharding import PartitionSpec as P

BOTH = ("grp", "vocab")
RING = 4
PIECES = ((0, 1792), (1792, 3584), (3584, 5120))
ORDERS = ("xyz", "yzx", "zxy")
BARRIERS = (4,)


def place_of(flat):
    grp, vocab = divmod(flat, 8)
    z_lo, rest = divmod(grp, 8)
    x, core = divmod(rest, 2)
    y, z_hi = divmod(vocab, 2)
    return {"x": x, "y": y, "z": z_hi * 2 + z_lo, "core": core}


def flat_of(at):
    grp = (at["z"] % 2) * 8 + at["x"] * 2 + at["core"]
    return grp * 8 + at["y"] * 2 + at["z"] // 2


def chip_turn(at, core):
    return (at - core) % RING


def meet_pairs(axis, bit):
    pairs = []
    for source in range(128):
        at = place_of(source)
        at[axis] = ((chip_turn(at[axis], at["core"]) ^ bit) + at["core"]) % RING
        pairs.append((source, flat_of(at)))
    return pairs


def swap_pairs(axis, distance, size):
    pairs = []
    for source in range(128):
        at = place_of(source)
        at[axis] = (at[axis] + distance) % size
        pairs.append((source, flat_of(at)))
    return pairs


FAR = {axis: meet_pairs(axis, 2) for axis in "xyz"}
NEAR = {axis: meet_pairs(axis, 1) for axis in "xyz"}
CORES = swap_pairs("core", 1, 2)
HALVES = swap_pairs("z", 2, RING)


def swap_cores(block):
    return lax.ppermute(block, BOTH, CORES)


def meet_gather(blocks):
    held = list(blocks)
    for turn in range(6):
        pairs = FAR if turn < 3 else NEAR
        taken = [
            lax.ppermute(part, BOTH, pairs[order[turn % 3]]) for part, order in zip(held, ORDERS)
        ]
        if turn == 5:
            return held, taken
        held = [jnp.stack(both) for both in zip(held, taken)]
        if turn in BARRIERS:
            held = list(lax.optimization_barrier(tuple(held)))


def weight_copies(k, own_w, other_w, weights, sems):
    a, b = PIECES[k]
    half = own_w.shape[1]
    rows = pl.ds(a, b - a)
    return [
        pltpu.make_async_copy(own_w.at[rows], weights[k].at[:, pl.ds(0, half)], sems.at[k, 0]),
        pltpu.make_async_copy(other_w.at[rows], weights[k].at[:, pl.ds(half, half)], sems.at[k, 1]),
    ]


def head_kernel(mark, *refs):
    parts, (own_w, other_w), refs = refs[:3], refs[3:5], refs[5:]
    if mark == 0:
        (out,), work = refs[:1], refs[1:]
    else:
        (before, own_out, other_out, sums), work = refs[:4], refs[4:]
    lhs, weights, (total, lhs_sem, w_sem, in_sem, out_sem) = work[0:3], work[3:6], work[6:]
    mine, cols = total.shape[4:]
    half = own_w.shape[1]

    def copies(k):
        part, room, sem = parts[k], lhs[k], lhs_sem.at[k]
        if k == 0:
            moves = [(part, room)]
        elif k == 1:
            moves = [(part.at[:, :, x], room.at[:, :, :, :, x]) for x in range(2)]
        else:
            moves = [
                (part.at[x, :, :, :, z], room.at[:, x, z]) for x in range(2) for z in range(2)
            ]
        return [
            pltpu.make_async_copy(source, to, sem.at[i]) for i, (source, to) in enumerate(moves)
        ] + weight_copies(k, own_w, other_w, weights, w_sem)

    for copy in copies(0):
        copy.start()
    if mark == 1:
        load = pltpu.make_async_copy(before, total, in_sem)
        load.start()
    for k in (1, 2):
        for copy in copies(k):
            copy.start()

    def product(k):
        for copy in copies(k):
            copy.wait()
        rows = lhs[k][...].reshape(32 * mine, -1)
        fresh = jnp.dot(rows, weights[k][...], preferred_element_type=jnp.float32)
        return fresh.reshape(2, 2, 8, mine, cols)

    fresh = product(0)
    if mark == 0:
        total[0] = fresh
        total[1] = jnp.zeros(total.shape[1:], jnp.float32)
    else:
        load.wait()
        total[1] += fresh
    total[:, :, mark] += product(1)
    total[:, mark] += product(2)

    def out_copies(z, y):
        if mark == 0:
            return [pltpu.make_async_copy(total.at[z, y], out.at[z, y], out_sem.at[z, y, 0])]
        return [
            pltpu.make_async_copy(
                total.at[z, y, :, :, :, pl.ds(at * half, half)], ref.at[z, y], out_sem.at[z, y, at]
            )
            for at, ref in enumerate((own_out, other_out))
        ]

    def finish(z, y):
        for copy in out_copies(z, y):
            copy.start()
        if mark == 1:
            rows = total[z, y].reshape(16 * mine, cols)
            top = jnp.max(rows, axis=1, keepdims=True)
            mass = jnp.sum(jnp.exp(rows - top), axis=1, keepdims=True)
            at = pl.ds(pl.multiple_of((z * 2 + y) * 16 * mine, 16 * mine), 16 * mine)
            sums[at] = top + jnp.log(mass)

    def both(z, carry):
        finish(z, 0)
        finish(z, 1)
        return carry

    lax.fori_loop(0, 2, both, 0)
    for z in range(2):
        for y in range(2):
            for copy in out_copies(z, y):
                copy.wait()


def head_logits(held, taken, own_w, other_w, mine):
    half = own_w.shape[1]
    rows = 64 * mine
    anywhere = pl.BlockSpec(memory_space=pl.ANY)
    widths = [b - a for a, b in PIECES]
    shape = (2, 2, 2, 8, mine)
    flops = rows * 5120 * 2 * half

    def call(mark, out_shape, out_specs, operands):
        return pl.pallas_call(
            functools.partial(head_kernel, mark),
            out_shape=out_shape,
            in_specs=[anywhere] * len(operands),
            out_specs=out_specs,
            scratch_shapes=[pltpu.VMEM((2, 2, 2, 2, 2, mine, w), jnp.bfloat16) for w in widths]
            + [pltpu.VMEM((w, 2 * half), jnp.bfloat16) for w in widths]
            + [
                pltpu.VMEM(shape + (2 * half,), jnp.float32),
                pltpu.SemaphoreType.DMA((3, 4)),
                pltpu.SemaphoreType.DMA((3, 2)),
                pltpu.SemaphoreType.DMA,
                pltpu.SemaphoreType.DMA((2, 2, 2)),
            ],
            compiler_params=pltpu.CompilerParams(vmem_limit_bytes=48 * 2**20),
            cost_estimate=pl.CostEstimate(
                flops=flops, bytes_accessed=26 * 10**6, transcendentals=mark * rows * 2 * half
            ),
            name=("head_early", "head_late")[mark],
        )(*operands)

    early = call(
        0,
        jax.ShapeDtypeStruct(shape + (2 * half,), jnp.float32),
        anywhere,
        held + [own_w, other_w],
    )
    return call(
        1,
        (
            jax.ShapeDtypeStruct(shape + (half,), jnp.float32),
            jax.ShapeDtypeStruct(shape + (half,), jnp.float32),
            jax.ShapeDtypeStruct((rows, 1), jnp.float32),
        ),
        (anywhere, anywhere, pl.BlockSpec(memory_space=pltpu.VMEM)),
        taken + [own_w, other_w, early],
    )


def front_kernel(
    prompts, column, embedded, gain, query_w, key_w, value_w, out, order, seen, raw, weights, sems
):
    samples, steps, width = embedded.shape
    cuts = (0, query_w.shape[1], query_w.shape[1] + key_w.shape[1])
    copies = [
        pltpu.make_async_copy(w, weights.at[:, pl.ds(at, w.shape[1])], sems.at[i])
        for i, (w, at) in enumerate(zip((query_w, key_w, value_w), cuts))
    ]
    for copy in copies:
        copy.start()
    for p in range(samples // 2):
        seen[p] = 0
    for i in range(samples):
        p = prompts[i]
        slot = p * 2 + seen[p]
        seen[p] = seen[p] + 1
        order[slot] = i
    for slot in range(samples):
        raw[slot * steps : (slot + 1) * steps] = embedded[order[slot]].astype(jnp.float32)
    rows = raw[...]
    mean_sq = jnp.mean(rows * rows, axis=-1, keepdims=True)
    normed = (rows * lax.rsqrt(mean_sq + 1e-06) * gain[...]).astype(jnp.bfloat16)
    span = out.shape[1] - weights.shape[1]
    at = pl.multiple_of(column[0], 128)
    out[:, weights.shape[1] :] = raw[:, pl.ds(at, span)].astype(jnp.bfloat16)
    for copy in copies:
        copy.wait()
    out[:, : weights.shape[1]] = jnp.dot(
        normed, weights[...], preferred_element_type=jnp.float32
    ).astype(jnp.bfloat16)


def front(sample_prompt, column, embedded, gain, query_w, key_w, value_w, span):
    samples, steps, width = embedded.shape
    anywhere = pl.BlockSpec(memory_space=pl.ANY)
    scalars = pl.BlockSpec(memory_space=pltpu.SMEM)
    vector = pl.BlockSpec(memory_space=pltpu.VMEM)
    cols = query_w.shape[1] + key_w.shape[1] + value_w.shape[1]
    return pl.pallas_call(
        front_kernel,
        out_shape=(
            jax.ShapeDtypeStruct((samples * steps, cols + span), jnp.bfloat16),
            jax.ShapeDtypeStruct((samples,), jnp.int32),
        ),
        in_specs=[scalars, scalars, vector, vector, anywhere, anywhere, anywhere],
        out_specs=(vector, scalars),
        scratch_shapes=[
            pltpu.SMEM((samples // 2,), jnp.int32),
            pltpu.VMEM((samples * steps, width), jnp.float32),
            pltpu.VMEM((width, cols), jnp.bfloat16),
            pltpu.SemaphoreType.DMA((3,)),
        ],
        compiler_params=pltpu.CompilerParams(vmem_limit_bytes=60 * 2**20),
        cost_estimate=pl.CostEstimate(
            flops=2 * samples * steps * width * cols, bytes_accessed=10**7, transcendentals=0
        ),
        name="front",
    )(sample_prompt, column, embedded, gain.reshape(1, -1), query_w, key_w, value_w)


def attend_kernel(steps, local, keys, values, out):
    head = keys.shape[1]
    rows = local.shape[0]
    groups = out.shape[1] // head
    scale = 1.0 / head**0.5
    new_keys = local[:, groups * head : (groups + 1) * head]
    new_values = local[:, (groups + 1) * head : (groups + 2) * head]
    at_row = lax.broadcasted_iota(jnp.int32, (rows, rows), 0)
    at_col = lax.broadcasted_iota(jnp.int32, (rows, rows), 1)
    seen = (at_row // steps == at_col // steps) & (at_col <= at_row)
    across = (((1,), (1,)), ((), ()))

    def parts(scores, value_rows):
        peak = jnp.max(scores, axis=1, keepdims=True)
        powers = jnp.exp(scores - peak)
        weighted = jnp.dot(
            powers.astype(jnp.bfloat16), value_rows, preferred_element_type=jnp.float32
        )
        return peak, jnp.sum(powers, axis=1, keepdims=True), weighted

    for g in range(groups):
        span = slice(g * head, (g + 1) * head)
        queries = local[:, span]
        scores = lax.dot_general(queries, keys[...], across, preferred_element_type=jnp.float32)
        prefix_peak, prefix_total, prefix_sum = parts(scores * scale, values[...])
        scores = lax.dot_general(queries, new_keys, across, preferred_element_type=jnp.float32)
        new_peak, new_total, new_sum = parts(jnp.where(seen, scores * scale, -1e30), new_values)
        peak = jnp.maximum(prefix_peak, new_peak)
        prefix_factor = jnp.exp(prefix_peak - peak)
        new_factor = jnp.exp(new_peak - peak)
        total = prefix_total * prefix_factor + new_total * new_factor
        attended = (prefix_sum * prefix_factor + new_sum * new_factor) / total
        out[:, span] = attended.astype(jnp.bfloat16)


def attend(local, keys, values, steps, cols):
    vector = pl.BlockSpec(memory_space=pltpu.VMEM)
    return pl.pallas_call(
        functools.partial(attend_kernel, steps),
        out_shape=jax.ShapeDtypeStruct((local.shape[0], cols), jnp.bfloat16),
        in_specs=[vector] * 3,
        out_specs=vector,
        compiler_params=pltpu.CompilerParams(vmem_limit_bytes=40 * 2**20),
        name="attend",
    )(local, keys, values)


def output_kernel(order, place, own, other, totals, out):
    pair = pl.program_id(0)
    y, z_hi = pair // 2, pair % 2
    core, x_here, y_here, z_here = place[0], place[1], place[2], place[3]
    for ref, plane in ((own, core), (other, 1 - core)):
        turn = lambda at: (at - plane) & 3
        apart = lambda here, there: turn(here) ^ turn(there)
        for z_lo in range(2):
            for x in range(4):
                prompt = z_lo * 8 + x * 2 + plane
                dz, dy, dx = apart(z_here, z_hi * 2 + z_lo), apart(y_here, y), apart(x_here, x)
                far = (dz >> 1) * 4 + (dy >> 1) * 2 + (dx >> 1)
                block = ref[dz & 1, dy & 1, dx & 1, far] - totals[prompt, pair]
                for row in range(4):
                    near, which = divmod(row, 2)
                    to = order[(pair * 2 + near) * 32 + prompt * 2 + which]
                    out[near * 32 + to] = block[row * 4 : row * 4 + 4]


def ordered_output(order, place, own, other, totals):
    width = own.shape[-1]
    whole = lambda a: pl.BlockSpec(a.shape, lambda i, *_: (0,) * a.ndim)
    return pl.pallas_call(
        output_kernel,
        out_shape=jax.ShapeDtypeStruct((512, 4, width), jnp.float32),
        grid_spec=pltpu.PrefetchScalarGridSpec(
            num_scalar_prefetch=2,
            grid=(8,),
            in_specs=[whole(own), whole(other), whole(totals)],
            out_specs=pl.BlockSpec((64, 4, width), lambda i, *_: (i, 0, 0)),
        ),
        compiler_params=pltpu.CompilerParams(vmem_limit_bytes=52 * 2**20),
        name="output",
    )(order, place, own, other, totals)


def rms_scale(rows, gain):
    mean_sq = jnp.mean(rows * rows, axis=-1, keepdims=True)
    return rows * lax.rsqrt(mean_sq + 1e-06) * gain


def log_sum(values, axis):
    top = jnp.max(values, axis=axis, keepdims=True)
    return jnp.squeeze(top, axis) + jnp.log(jnp.sum(jnp.exp(values - top), axis=axis))


def spread(values, axis):
    copies = lax.axis_size(axis)
    return lax.all_to_all(
        jnp.broadcast_to(values[None], (copies,) + values.shape), axis, 0, 0, tiled=True
    )


def on_device(
    embedded,
    attn_gain,
    query_weight,
    key_weight,
    value_weight,
    out_weight,
    final_gain,
    head_weight,
    prefix_keys,
    prefix_values,
    sample_prompt,
):
    samples, steps, width = embedded.shape
    rows = samples * steps
    cols = query_weight.shape[1]
    core = lax.axis_index("grp") % 2
    z_hi = lax.axis_index("vocab") % 2
    z = z_hi * 2 + lax.axis_index("grp") // 8
    y = lax.axis_index("vocab") // 2
    x = (lax.axis_index("grp") // 2) % 4
    shares = lax.axis_size("vocab")
    mine = rows // shares
    span = width // shares
    half = width // 2
    other_weight = swap_cores(head_weight)

    own_columns = lax.axis_index("vocab") * span
    sorted_rows, sample_at = front(
        sample_prompt,
        own_columns.reshape(1).astype(jnp.int32),
        embedded,
        attn_gain,
        query_weight,
        key_weight,
        value_weight,
        span,
    )
    local = lax.all_to_all(sorted_rows, "grp", 0, 0, tiled=True)

    attended = attend(local, prefix_keys[0, 0], prefix_values[0, 0], steps, cols)
    attended, other_weight = lax.optimization_barrier((attended, other_weight))
    own_embedded = local[:, -span:].astype(jnp.float32)

    def product(part, attended):
        w = lax.slice_in_dim(out_weight, part * half, (part + 1) * half, axis=1)
        full = jnp.dot(attended, w, preferred_element_type=jnp.float32)
        at = (y * 2 + z_hi) % 4 * span
        chunk = lax.dynamic_slice_in_dim(full, at, span, 1)
        chunk = jnp.where((y * 2 + z_hi) // 4 == part, chunk + own_embedded, chunk)
        return lax.dynamic_update_slice_in_dim(full, chunk, at, 1)

    along_y = [[at * 2 + z_at for at in range(4)] for z_at in range(2)]

    def over_y(block):
        return lax.all_to_all(block, "vocab", 0, 0, tiled=True, axis_index_groups=along_y)

    def over_z(block, axis):
        kept = lax.dynamic_index_in_dim(block, z_hi, axis, False)
        given = lax.dynamic_index_in_dim(block, 1 - z_hi, axis, False)
        return kept, lax.ppermute(given, BOTH, HALVES)

    second, attended = lax.optimization_barrier((product(1, attended), attended))
    kept, taken = over_z(second.reshape(4, 2, mine, half), 1)
    first_y = over_y(product(0, attended)).reshape(4, 2, mine, half)
    first_y, second_z = lax.optimization_barrier((first_y, kept + taken))
    kept, taken = over_z(jnp.sum(first_y, axis=0), 0)
    second_y = jnp.sum(over_y(second_z.reshape(4 * mine, half)).reshape(4, mine, half), axis=0)
    hidden = jnp.concatenate([kept + taken, second_y], axis=1)
    normed = rms_scale(hidden, final_gain).astype(jnp.bfloat16)

    held, taken = meet_gather([normed[:, a:b] for a, b in PIECES])
    logits, other_logits, local_sum = head_logits(held, taken, head_weight, other_weight, mine)
    crossed = swap_cores(other_logits)

    places = jnp.arange(RING, dtype=jnp.int32)
    apart = lambda at: chip_turn(at, core) ^ chip_turn(places, core)
    dz, dy, dx = apart(z)[:, None, None], apart(y)[None, :, None], apart(x)[None, None, :]
    nears = (dz & 1) * 4 + (dy & 1) * 2 + (dx & 1)
    fars = (dz >> 1) * 4 + (dy >> 1) * 2 + (dx >> 1)
    mine_order = (nears * 8 + fars).reshape(64)
    local_sum = jnp.take(local_sum.reshape(64, mine), mine_order, axis=0)
    over_vocab = log_sum(spread(local_sum.reshape(64 * mine), "vocab"), 0)
    sent = jnp.concatenate([over_vocab, sample_at.astype(jnp.float32)])
    over_grp = spread(sent, "grp")
    order = over_grp[:, 64 * mine :].astype(jnp.int32).reshape(-1)
    total = log_sum(over_grp[:, : 64 * mine].reshape(8, 2, 64 * mine), 0)
    total = total.reshape(2, 2, 2, 4, 4, mine).transpose(2, 4, 0, 3, 1, 5)
    return ordered_output(
        order,
        jnp.stack([core, x, y, z]).astype(jnp.int32),
        logits,
        crossed,
        total.reshape(16, 8, mine, 1),
    )


def solution(mesh):
    placed = (
        P("grp", None, None),
        P(),
        P(None, "vocab"),
        P(None, "vocab"),
        P(None, "vocab"),
        P("vocab", None),
        P(),
        P(None, ("grp", "vocab")),
        P("grp", "vocab", None, None),
        P("grp", "vocab", None, None),
        P("grp"),
    )
    return jax.shard_map(
        on_device,
        mesh=mesh,
        in_specs=placed,
        out_specs=P(None, None, ("grp", "vocab")),
        check_vma=False,
    )
```

```python
import functools

import jax
import jax.numpy as jnp
from jax import lax
from jax.experimental import pallas as pl
from jax.experimental.pallas import tpu as pltpu
from jax.sharding import PartitionSpec as P

BOTH = ("grp", "vocab")
RING = 4
PIECES = ((0, 1792), (1792, 3584), (3584, 5120))
ORDERS = ("xyz", "yzx", "zxy")


def place_of(flat):
    grp, vocab = divmod(flat, 8)
    z_lo, rest = divmod(grp, 8)
    x, core = divmod(rest, 2)
    y, z_hi = divmod(vocab, 2)
    return {"x": x, "y": y, "z": z_hi * 2 + z_lo, "core": core}


def flat_of(at):
    grp = (at["z"] % 2) * 8 + at["x"] * 2 + at["core"]
    return grp * 8 + at["y"] * 2 + at["z"] // 2


def chip_turn(at, core):
    return (at - core) % RING


def meet_pairs(axis, bit):
    pairs = []
    for source in range(128):
        at = place_of(source)
        at[axis] = ((chip_turn(at[axis], at["core"]) ^ bit) + at["core"]) % RING
        pairs.append((source, flat_of(at)))
    return pairs


def swap_pairs(axis, distance, size):
    pairs = []
    for source in range(128):
        at = place_of(source)
        at[axis] = (at[axis] + distance) % size
        pairs.append((source, flat_of(at)))
    return pairs


FAR = {axis: meet_pairs(axis, 2) for axis in "xyz"}
NEAR = {axis: meet_pairs(axis, 1) for axis in "xyz"}
CORES = swap_pairs("core", 1, 2)
HALVES = swap_pairs("z", 2, RING)


def swap_cores(block):
    return lax.ppermute(block, BOTH, CORES)


def meet_gather(blocks):
    held = list(blocks)

    def meet(parts, turn):
        pairs = FAR if turn < 3 else NEAR
        return [
            lax.ppermute(part, BOTH, pairs[order[turn % 3]]) for part, order in zip(parts, ORDERS)
        ]

    for turn in range(4):
        held = [jnp.stack(both) for both in zip(held, meet(held, turn))]
    fifth = meet(held, 4)
    sixth = meet(held, 5)
    fifth = list(lax.optimization_barrier(tuple(fifth)))
    return list(zip(held, fifth)), list(zip(sixth, meet(fifth, 5)))


def weight_copies(k, own_w, other_w, weights, sems):
    a, b = PIECES[k]
    half = own_w.shape[1]
    rows = pl.ds(a, b - a)
    return [
        pltpu.make_async_copy(own_w.at[rows], weights[k].at[:, pl.ds(0, half)], sems.at[k, 0]),
        pltpu.make_async_copy(other_w.at[rows], weights[k].at[:, pl.ds(half, half)], sems.at[k, 1]),
    ]


def head_kernel(mark, *refs):
    parts, (own_w, other_w), refs = (refs[0:2], refs[2:4], refs[4:6]), refs[6:8], refs[8:]
    if mark == 0:
        (out,), work = refs[:1], refs[1:]
    else:
        (before, own_out, other_out, sums), work = refs[:4], refs[4:]
    lhs, weights, (total, lhs_sem, w_sem, in_sem, out_sem) = work[0:3], work[3:6], work[6:]
    mine, cols = total.shape[4:]
    half = own_w.shape[1]

    def copies(k):
        room, sem = lhs[k], lhs_sem.at[k]
        moves = []
        for h, part in enumerate(parts[k]):
            if k == 0:
                moves.append((part, room.at[h]))
            elif k == 1:
                moves += [(part.at[:, x], room.at[h, :, :, :, x]) for x in range(2)]
            else:
                moves += [(part.at[:, :, :, z], room.at[:, h, z]) for z in range(2)]
        return [
            pltpu.make_async_copy(source, to, sem.at[i]) for i, (source, to) in enumerate(moves)
        ] + weight_copies(k, own_w, other_w, weights, w_sem)

    def begin(k):
        for copy in copies(k):
            copy.start()

    def product(k):
        for copy in copies(k):
            copy.wait()
        if k < 2:
            begin(k + 1)
        rows = lhs[k][...].reshape(32 * mine, -1)
        fresh = jnp.dot(rows, weights[k][...], preferred_element_type=jnp.float32)
        return fresh.reshape(2, 2, 8, mine, cols)

    begin(0)
    if mark == 0:
        total[0] = product(0)
        total[1] = jnp.zeros(total.shape[1:], jnp.float32)
    else:
        load = pltpu.make_async_copy(before, total, in_sem)
        load.start()
        fresh = product(0)
        load.wait()
        total[1] += fresh
    def out_copies(z, y):
        if mark == 0:
            return [pltpu.make_async_copy(total.at[z, y], out.at[z, y], out_sem.at[z, y, 0])]
        return [
            pltpu.make_async_copy(
                total.at[z, y, :, :, :, pl.ds(at * half, half)], ref.at[z, y], out_sem.at[z, y, at]
            )
            for at, ref in enumerate((own_out, other_out))
        ]

    def finish(z, y):
        for copy in out_copies(z, y):
            copy.start()
        if mark == 1:
            rows = total[z, y].reshape(16 * mine, cols)
            top = jnp.max(rows, axis=1, keepdims=True)
            mass = jnp.sum(jnp.exp(rows - top), axis=1, keepdims=True)
            at = pl.ds(pl.multiple_of((z * 2 + y) * 16 * mine, 16 * mine), 16 * mine)
            sums[at] = top + jnp.log(mass)

    total[:, :, mark] += product(1)
    for z in range(2):
        finish(z, 1 - mark)
    total[:, mark] += product(2)
    for z in range(2):
        finish(z, mark)
    for z in range(2):
        for y in range(2):
            for copy in out_copies(z, y):
                copy.wait()


def head_logits(held, taken, own_w, other_w, mine):
    half = own_w.shape[1]
    rows = 64 * mine
    anywhere = pl.BlockSpec(memory_space=pl.ANY)
    widths = [b - a for a, b in PIECES]
    shape = (2, 2, 2, 8, mine)
    flops = rows * 5120 * 2 * half

    def call(mark, out_shape, out_specs, operands):
        return pl.pallas_call(
            functools.partial(head_kernel, mark),
            out_shape=out_shape,
            in_specs=[anywhere] * len(operands),
            out_specs=out_specs,
            scratch_shapes=[pltpu.VMEM((2, 2, 2, 2, 2, mine, w), jnp.bfloat16) for w in widths]
            + [pltpu.VMEM((w, 2 * half), jnp.bfloat16) for w in widths]
            + [
                pltpu.VMEM(shape + (2 * half,), jnp.float32),
                pltpu.SemaphoreType.DMA((3, 4)),
                pltpu.SemaphoreType.DMA((3, 2)),
                pltpu.SemaphoreType.DMA,
                pltpu.SemaphoreType.DMA((2, 2, 2)),
            ],
            compiler_params=pltpu.CompilerParams(vmem_limit_bytes=48 * 2**20),
            cost_estimate=pl.CostEstimate(
                flops=flops, bytes_accessed=26 * 10**6, transcendentals=mark * rows * 2 * half
            ),
            name=("head_early", "head_late")[mark],
        )(*operands)

    early = call(
        0,
        jax.ShapeDtypeStruct(shape + (2 * half,), jnp.float32),
        anywhere,
        [half for piece in held for half in piece] + [own_w, other_w],
    )
    return call(
        1,
        (
            jax.ShapeDtypeStruct(shape + (half,), jnp.float32),
            jax.ShapeDtypeStruct(shape + (half,), jnp.float32),
            jax.ShapeDtypeStruct((rows, 1), jnp.float32),
        ),
        (anywhere, anywhere, pl.BlockSpec(memory_space=pltpu.VMEM)),
        [half for piece in taken for half in piece] + [own_w, other_w, early],
    )


def front_kernel(
    prompts, column, embedded, gain, query_w, key_w, value_w, out, order, seen, raw, weights, sems
):
    samples, steps, width = embedded.shape
    cuts = (0, query_w.shape[1], query_w.shape[1] + key_w.shape[1])
    copies = [
        pltpu.make_async_copy(w, weights.at[:, pl.ds(at, w.shape[1])], sems.at[i])
        for i, (w, at) in enumerate(zip((query_w, key_w, value_w), cuts))
    ]
    for copy in copies:
        copy.start()
    for p in range(samples // 2):
        seen[p] = 0
    for i in range(samples):
        p = prompts[i]
        slot = p * 2 + seen[p]
        seen[p] = seen[p] + 1
        order[slot] = i
    for slot in range(samples):
        raw[slot * steps : (slot + 1) * steps] = embedded[order[slot]].astype(jnp.float32)
    rows = raw[...]
    mean_sq = jnp.mean(rows * rows, axis=-1, keepdims=True)
    normed = (rows * lax.rsqrt(mean_sq + 1e-06) * gain[...]).astype(jnp.bfloat16)
    span = out.shape[1] - weights.shape[1]
    at = pl.multiple_of(column[0], 128)
    out[:, weights.shape[1] :] = raw[:, pl.ds(at, span)].astype(jnp.bfloat16)
    for copy in copies:
        copy.wait()
    out[:, : weights.shape[1]] = jnp.dot(
        normed, weights[...], preferred_element_type=jnp.float32
    ).astype(jnp.bfloat16)


def front(sample_prompt, column, embedded, gain, query_w, key_w, value_w, span):
    samples, steps, width = embedded.shape
    anywhere = pl.BlockSpec(memory_space=pl.ANY)
    scalars = pl.BlockSpec(memory_space=pltpu.SMEM)
    vector = pl.BlockSpec(memory_space=pltpu.VMEM)
    cols = query_w.shape[1] + key_w.shape[1] + value_w.shape[1]
    return pl.pallas_call(
        front_kernel,
        out_shape=(
            jax.ShapeDtypeStruct((samples * steps, cols + span), jnp.bfloat16),
            jax.ShapeDtypeStruct((samples,), jnp.int32),
        ),
        in_specs=[scalars, scalars, vector, vector, anywhere, anywhere, anywhere],
        out_specs=(vector, scalars),
        scratch_shapes=[
            pltpu.SMEM((samples // 2,), jnp.int32),
            pltpu.VMEM((samples * steps, width), jnp.float32),
            pltpu.VMEM((width, cols), jnp.bfloat16),
            pltpu.SemaphoreType.DMA((3,)),
        ],
        compiler_params=pltpu.CompilerParams(vmem_limit_bytes=60 * 2**20),
        cost_estimate=pl.CostEstimate(
            flops=2 * samples * steps * width * cols, bytes_accessed=10**7, transcendentals=0
        ),
        name="front",
    )(sample_prompt, column, embedded, gain.reshape(1, -1), query_w, key_w, value_w)


def attend_kernel(steps, local, keys, values, out):
    head = keys.shape[1]
    rows = local.shape[0]
    groups = out.shape[1] // head
    scale = 1.0 / head**0.5
    new_keys = local[:, groups * head : (groups + 1) * head]
    new_values = local[:, (groups + 1) * head : (groups + 2) * head]
    at_row = lax.broadcasted_iota(jnp.int32, (rows, rows), 0)
    at_col = lax.broadcasted_iota(jnp.int32, (rows, rows), 1)
    seen = (at_row // steps == at_col // steps) & (at_col <= at_row)
    across = (((1,), (1,)), ((), ()))

    def parts(scores, value_rows):
        peak = jnp.max(scores, axis=1, keepdims=True)
        powers = jnp.exp(scores - peak)
        weighted = jnp.dot(
            powers.astype(jnp.bfloat16), value_rows, preferred_element_type=jnp.float32
        )
        return peak, jnp.sum(powers, axis=1, keepdims=True), weighted

    for g in range(groups):
        span = slice(g * head, (g + 1) * head)
        queries = local[:, span]
        scores = lax.dot_general(queries, keys[...], across, preferred_element_type=jnp.float32)
        prefix_peak, prefix_total, prefix_sum = parts(scores * scale, values[...])
        scores = lax.dot_general(queries, new_keys, across, preferred_element_type=jnp.float32)
        new_peak, new_total, new_sum = parts(jnp.where(seen, scores * scale, -1e30), new_values)
        peak = jnp.maximum(prefix_peak, new_peak)
        prefix_factor = jnp.exp(prefix_peak - peak)
        new_factor = jnp.exp(new_peak - peak)
        total = prefix_total * prefix_factor + new_total * new_factor
        attended = (prefix_sum * prefix_factor + new_sum * new_factor) / total
        out[:, span] = attended.astype(jnp.bfloat16)


def attend(local, keys, values, steps, cols):
    vector = pl.BlockSpec(memory_space=pltpu.VMEM)
    return pl.pallas_call(
        functools.partial(attend_kernel, steps),
        out_shape=jax.ShapeDtypeStruct((local.shape[0], cols), jnp.bfloat16),
        in_specs=[vector] * 3,
        out_specs=vector,
        compiler_params=pltpu.CompilerParams(vmem_limit_bytes=40 * 2**20),
        name="attend",
    )(local, keys, values)


def output_kernel(order, place, own, other, totals, out):
    pair = pl.program_id(0)
    y, z_hi = pair // 2, pair % 2
    core, x_here, y_here, z_here = place[0], place[1], place[2], place[3]
    for ref, plane in ((own, core), (other, 1 - core)):
        turn = lambda at: (at - plane) & 3
        apart = lambda here, there: turn(here) ^ turn(there)
        for z_lo in range(2):
            for x in range(4):
                prompt = z_lo * 8 + x * 2 + plane
                dz, dy, dx = apart(z_here, z_hi * 2 + z_lo), apart(y_here, y), apart(x_here, x)
                far = (dz >> 1) * 4 + (dy >> 1) * 2 + (dx >> 1)
                block = ref[dz & 1, dy & 1, dx & 1, far] - totals[prompt, pair]
                for row in range(4):
                    near, which = divmod(row, 2)
                    to = order[(pair * 2 + near) * 32 + prompt * 2 + which]
                    out[near * 32 + to] = block[row * 4 : row * 4 + 4]


def ordered_output(order, place, own, other, totals):
    width = own.shape[-1]
    whole = lambda a: pl.BlockSpec(a.shape, lambda i, *_: (0,) * a.ndim)
    return pl.pallas_call(
        output_kernel,
        out_shape=jax.ShapeDtypeStruct((512, 4, width), jnp.float32),
        grid_spec=pltpu.PrefetchScalarGridSpec(
            num_scalar_prefetch=2,
            grid=(8,),
            in_specs=[whole(own), whole(other), whole(totals)],
            out_specs=pl.BlockSpec((64, 4, width), lambda i, *_: (i, 0, 0)),
        ),
        compiler_params=pltpu.CompilerParams(vmem_limit_bytes=52 * 2**20),
        name="output",
    )(order, place, own, other, totals)


def rms_scale(rows, gain):
    mean_sq = jnp.mean(rows * rows, axis=-1, keepdims=True)
    return rows * lax.rsqrt(mean_sq + 1e-06) * gain


def log_sum(values, axis):
    top = jnp.max(values, axis=axis, keepdims=True)
    return jnp.squeeze(top, axis) + jnp.log(jnp.sum(jnp.exp(values - top), axis=axis))


def spread(values, axis):
    copies = lax.axis_size(axis)
    return lax.all_to_all(
        jnp.broadcast_to(values[None], (copies,) + values.shape), axis, 0, 0, tiled=True
    )


def on_device(
    embedded,
    attn_gain,
    query_weight,
    key_weight,
    value_weight,
    out_weight,
    final_gain,
    head_weight,
    prefix_keys,
    prefix_values,
    sample_prompt,
):
    samples, steps, width = embedded.shape
    rows = samples * steps
    cols = query_weight.shape[1]
    core = lax.axis_index("grp") % 2
    z_hi = lax.axis_index("vocab") % 2
    z = z_hi * 2 + lax.axis_index("grp") // 8
    y = lax.axis_index("vocab") // 2
    x = (lax.axis_index("grp") // 2) % 4
    shares = lax.axis_size("vocab")
    mine = rows // shares
    span = width // shares
    half = width // 2
    other_weight = swap_cores(head_weight)

    own_columns = lax.axis_index("vocab") * span
    sorted_rows, sample_at = front(
        sample_prompt,
        own_columns.reshape(1).astype(jnp.int32),
        embedded,
        attn_gain,
        query_weight,
        key_weight,
        value_weight,
        span,
    )
    local = lax.all_to_all(sorted_rows, "grp", 0, 0, tiled=True)

    attended = attend(local, prefix_keys[0, 0], prefix_values[0, 0], steps, cols)
    attended, other_weight = lax.optimization_barrier((attended, other_weight))
    own_embedded = local[:, -span:].astype(jnp.float32)

    def product(part, attended):
        w = lax.slice_in_dim(out_weight, part * half, (part + 1) * half, axis=1)
        full = jnp.dot(attended, w, preferred_element_type=jnp.float32)
        at = (y * 2 + z_hi) % 4 * span
        chunk = lax.dynamic_slice_in_dim(full, at, span, 1)
        chunk = jnp.where((y * 2 + z_hi) // 4 == part, chunk + own_embedded, chunk)
        return lax.dynamic_update_slice_in_dim(full, chunk, at, 1)

    both = jnp.concatenate([product(0, attended), product(1, attended)], axis=1)
    arrived = lax.all_to_all(both, "vocab", 0, 0, tiled=True)
    hidden = jnp.sum(arrived.reshape(shares, mine, width), axis=0)
    normed = rms_scale(hidden, final_gain).astype(jnp.bfloat16)

    held, taken = meet_gather([normed[:, a:b] for a, b in PIECES])
    logits, other_logits, local_sum = head_logits(held, taken, head_weight, other_weight, mine)
    crossed = swap_cores(other_logits)

    places = jnp.arange(RING, dtype=jnp.int32)
    apart = lambda at: chip_turn(at, core) ^ chip_turn(places, core)
    dz, dy, dx = apart(z)[:, None, None], apart(y)[None, :, None], apart(x)[None, None, :]
    nears = (dz & 1) * 4 + (dy & 1) * 2 + (dx & 1)
    fars = (dz >> 1) * 4 + (dy >> 1) * 2 + (dx >> 1)
    mine_order = (nears * 8 + fars).reshape(64)
    local_sum = jnp.take(local_sum.reshape(64, mine), mine_order, axis=0)
    over_vocab = log_sum(spread(local_sum.reshape(64 * mine), "vocab"), 0)
    sent = jnp.concatenate([over_vocab, sample_at.astype(jnp.float32)])
    over_grp = spread(sent, "grp")
    order = over_grp[:, 64 * mine :].astype(jnp.int32).reshape(-1)
    total = log_sum(over_grp[:, : 64 * mine].reshape(8, 2, 64 * mine), 0)
    total = total.reshape(2, 2, 2, 4, 4, mine).transpose(2, 4, 0, 3, 1, 5)
    return ordered_output(
        order,
        jnp.stack([core, x, y, z]).astype(jnp.int32),
        logits,
        crossed,
        total.reshape(16, 8, mine, 1),
    )


def solution(mesh):
    placed = (
        P("grp", None, None),
        P(),
        P(None, "vocab"),
        P(None, "vocab"),
        P(None, "vocab"),
        P("vocab", None),
        P(),
        P(None, ("grp", "vocab")),
        P("grp", "vocab", None, None),
        P("grp", "vocab", None, None),
        P("grp"),
    )
    return jax.shard_map(
        on_device,
        mesh=mesh,
        in_specs=placed,
        out_specs=P(None, None, ("grp", "vocab")),
        check_vma=False,
    )
```

```python
import functools

import jax
import jax.numpy as jnp
from jax import lax
from jax.experimental import pallas as pl
from jax.experimental.pallas import tpu as pltpu
from jax.sharding import PartitionSpec as P

BOTH = ("grp", "vocab")
RING = 4
PIECES = ((0, 1536), (1536, 3328), (3328, 5120))
ORDERS = ("xyz", "yzx", "zxy")


def place_of(flat):
    grp, vocab = divmod(flat, 8)
    z_lo, rest = divmod(grp, 8)
    x, core = divmod(rest, 2)
    y, z_hi = divmod(vocab, 2)
    return {"x": x, "y": y, "z": z_hi * 2 + z_lo, "core": core}


def flat_of(at):
    grp = (at["z"] % 2) * 8 + at["x"] * 2 + at["core"]
    return grp * 8 + at["y"] * 2 + at["z"] // 2


def chip_turn(at, core):
    return (at - core) % RING


def meet_pairs(axis, bit):
    pairs = []
    for source in range(128):
        at = place_of(source)
        at[axis] = ((chip_turn(at[axis], at["core"]) ^ bit) + at["core"]) % RING
        pairs.append((source, flat_of(at)))
    return pairs


def swap_pairs(axis, distance, size):
    pairs = []
    for source in range(128):
        at = place_of(source)
        at[axis] = (at[axis] + distance) % size
        pairs.append((source, flat_of(at)))
    return pairs


FAR = {axis: meet_pairs(axis, 2) for axis in "xyz"}
NEAR = {axis: meet_pairs(axis, 1) for axis in "xyz"}
CORES = swap_pairs("core", 1, 2)
HALVES = swap_pairs("z", 2, RING)


def swap_cores(block):
    return lax.ppermute(block, BOTH, CORES)


def meet_gather(blocks):
    held = list(blocks)

    def meet(parts, turn):
        pairs = FAR if turn < 3 else NEAR
        return [
            lax.ppermute(part, BOTH, pairs[order[turn % 3]]) for part, order in zip(parts, ORDERS)
        ]

    for turn in range(4):
        held = [jnp.stack(both) for both in zip(held, meet(held, turn))]
    fifth = meet(held, 4)
    sixth = meet(held, 5)
    fifth = list(lax.optimization_barrier(tuple(fifth)))
    return list(zip(held, fifth)), list(zip(sixth, meet(fifth, 5)))


def weight_copies(k, own_w, other_w, weights, sems):
    a, b = PIECES[k]
    half = own_w.shape[1]
    rows = pl.ds(a, b - a)
    return [
        pltpu.make_async_copy(own_w.at[rows], weights[k].at[:, pl.ds(0, half)], sems.at[k, 0]),
        pltpu.make_async_copy(other_w.at[rows], weights[k].at[:, pl.ds(half, half)], sems.at[k, 1]),
    ]


def head_kernel(mark, *refs):
    parts, (own_w, other_w), refs = (refs[0:2], refs[2:4], refs[4:6]), refs[6:8], refs[8:]
    if mark == 0:
        (out,), work = refs[:1], refs[1:]
    else:
        (before, own_out, other_out, sums), work = refs[:4], refs[4:]
    lhs, weights, (total, lhs_sem, w_sem, in_sem, out_sem) = work[0:3], work[3:6], work[6:]
    mine, cols = total.shape[4:]
    half = own_w.shape[1]

    def copies(k):
        room, sem = lhs[k], lhs_sem.at[k]
        moves = []
        for h, part in enumerate(parts[k]):
            if k == 0:
                moves.append((part, room.at[h]))
            elif k == 1:
                moves += [(part.at[:, x], room.at[h, :, :, :, x]) for x in range(2)]
            else:
                moves += [(part.at[:, :, :, z], room.at[:, h, z]) for z in range(2)]
        return [
            pltpu.make_async_copy(source, to, sem.at[i]) for i, (source, to) in enumerate(moves)
        ] + weight_copies(k, own_w, other_w, weights, w_sem)

    def begin(k):
        for copy in copies(k):
            copy.start()

    def product(k):
        for copy in copies(k):
            copy.wait()
        if k < 2:
            begin(k + 1)
        rows = lhs[k][...].reshape(32 * mine, -1)
        fresh = jnp.dot(rows, weights[k][...], preferred_element_type=jnp.float32)
        return fresh.reshape(2, 2, 8, mine, cols)

    begin(0)
    if mark == 0:
        total[0] = product(0)
        total[1] = jnp.zeros(total.shape[1:], jnp.float32)
    else:
        load = pltpu.make_async_copy(before, total, in_sem)
        load.start()
        fresh = product(0)
        load.wait()
        total[1] += fresh
    def out_copies(z, y):
        if mark == 0:
            return [pltpu.make_async_copy(total.at[z, y], out.at[z, y], out_sem.at[z, y, 0])]
        return [
            pltpu.make_async_copy(
                total.at[z, y, :, :, :, pl.ds(at * half, half)], ref.at[z, y], out_sem.at[z, y, at]
            )
            for at, ref in enumerate((own_out, other_out))
        ]

    def finish(z, y):
        for copy in out_copies(z, y):
            copy.start()
        if mark == 1:
            rows = total[z, y].reshape(16 * mine, cols)
            top = jnp.max(rows, axis=1, keepdims=True)
            mass = jnp.sum(jnp.exp(rows - top), axis=1, keepdims=True)
            at = pl.ds(pl.multiple_of((z * 2 + y) * 16 * mine, 16 * mine), 16 * mine)
            sums[at] = top + jnp.log(mass)

    total[:, :, mark] += product(1)
    for z in range(2):
        finish(z, 1 - mark)
    total[:, mark] += product(2)
    for z in range(2):
        finish(z, mark)
    for z in range(2):
        for y in range(2):
            for copy in out_copies(z, y):
                copy.wait()


def head_logits(held, taken, own_w, other_w, mine):
    half = own_w.shape[1]
    rows = 64 * mine
    anywhere = pl.BlockSpec(memory_space=pl.ANY)
    widths = [b - a for a, b in PIECES]
    shape = (2, 2, 2, 8, mine)
    flops = rows * 5120 * 2 * half

    def call(mark, out_shape, out_specs, operands):
        return pl.pallas_call(
            functools.partial(head_kernel, mark),
            out_shape=out_shape,
            in_specs=[anywhere] * len(operands),
            out_specs=out_specs,
            scratch_shapes=[pltpu.VMEM((2, 2, 2, 2, 2, mine, w), jnp.bfloat16) for w in widths]
            + [pltpu.VMEM((w, 2 * half), jnp.bfloat16) for w in widths]
            + [
                pltpu.VMEM(shape + (2 * half,), jnp.float32),
                pltpu.SemaphoreType.DMA((3, 4)),
                pltpu.SemaphoreType.DMA((3, 2)),
                pltpu.SemaphoreType.DMA,
                pltpu.SemaphoreType.DMA((2, 2, 2)),
            ],
            compiler_params=pltpu.CompilerParams(vmem_limit_bytes=48 * 2**20),
            cost_estimate=pl.CostEstimate(
                flops=flops, bytes_accessed=26 * 10**6, transcendentals=mark * rows * 2 * half
            ),
            name=("head_early", "head_late")[mark],
        )(*operands)

    early = call(
        0,
        jax.ShapeDtypeStruct(shape + (2 * half,), jnp.float32),
        anywhere,
        [half for piece in held for half in piece] + [own_w, other_w],
    )
    return call(
        1,
        (
            jax.ShapeDtypeStruct(shape + (half,), jnp.float32),
            jax.ShapeDtypeStruct(shape + (half,), jnp.float32),
            jax.ShapeDtypeStruct((rows, 1), jnp.float32),
        ),
        (anywhere, anywhere, pl.BlockSpec(memory_space=pltpu.VMEM)),
        [half for piece in taken for half in piece] + [own_w, other_w, early],
    )


def front_kernel(
    prompts, column, embedded, gain, query_w, key_w, value_w, out, order, seen, raw, weights, sems
):
    samples, steps, width = embedded.shape
    cuts = (0, query_w.shape[1], query_w.shape[1] + key_w.shape[1])
    copies = [
        pltpu.make_async_copy(w, weights.at[:, pl.ds(at, w.shape[1])], sems.at[i])
        for i, (w, at) in enumerate(zip((query_w, key_w, value_w), cuts))
    ]
    for copy in copies:
        copy.start()
    for p in range(samples // 2):
        seen[p] = 0
    for i in range(samples):
        p = prompts[i]
        slot = p * 2 + seen[p]
        seen[p] = seen[p] + 1
        order[slot] = i
    for slot in range(samples):
        raw[slot * steps : (slot + 1) * steps] = embedded[order[slot]].astype(jnp.float32)
    rows = raw[...]
    mean_sq = jnp.mean(rows * rows, axis=-1, keepdims=True)
    normed = (rows * lax.rsqrt(mean_sq + 1e-06) * gain[...]).astype(jnp.bfloat16)
    span = out.shape[1] - weights.shape[1]
    at = pl.multiple_of(column[0], 128)
    out[:, weights.shape[1] :] = raw[:, pl.ds(at, span)].astype(jnp.bfloat16)
    for copy in copies:
        copy.wait()
    out[:, : weights.shape[1]] = jnp.dot(
        normed, weights[...], preferred_element_type=jnp.float32
    ).astype(jnp.bfloat16)


def front(sample_prompt, column, embedded, gain, query_w, key_w, value_w, span):
    samples, steps, width = embedded.shape
    anywhere = pl.BlockSpec(memory_space=pl.ANY)
    scalars = pl.BlockSpec(memory_space=pltpu.SMEM)
    vector = pl.BlockSpec(memory_space=pltpu.VMEM)
    cols = query_w.shape[1] + key_w.shape[1] + value_w.shape[1]
    return pl.pallas_call(
        front_kernel,
        out_shape=(
            jax.ShapeDtypeStruct((samples * steps, cols + span), jnp.bfloat16),
            jax.ShapeDtypeStruct((samples,), jnp.int32),
        ),
        in_specs=[scalars, scalars, vector, vector, anywhere, anywhere, anywhere],
        out_specs=(vector, scalars),
        scratch_shapes=[
            pltpu.SMEM((samples // 2,), jnp.int32),
            pltpu.VMEM((samples * steps, width), jnp.float32),
            pltpu.VMEM((width, cols), jnp.bfloat16),
            pltpu.SemaphoreType.DMA((3,)),
        ],
        compiler_params=pltpu.CompilerParams(vmem_limit_bytes=60 * 2**20),
        cost_estimate=pl.CostEstimate(
            flops=2 * samples * steps * width * cols, bytes_accessed=10**7, transcendentals=0
        ),
        name="front",
    )(sample_prompt, column, embedded, gain.reshape(1, -1), query_w, key_w, value_w)


def attend_kernel(steps, local, keys, values, out):
    head = keys.shape[1]
    rows = local.shape[0]
    groups = out.shape[1] // head
    scale = 1.0 / head**0.5
    new_keys = local[:, groups * head : (groups + 1) * head]
    new_values = local[:, (groups + 1) * head : (groups + 2) * head]
    at_row = lax.broadcasted_iota(jnp.int32, (rows, rows), 0)
    at_col = lax.broadcasted_iota(jnp.int32, (rows, rows), 1)
    seen = (at_row // steps == at_col // steps) & (at_col <= at_row)
    across = (((1,), (1,)), ((), ()))

    def parts(scores, value_rows):
        peak = jnp.max(scores, axis=1, keepdims=True)
        powers = jnp.exp(scores - peak)
        weighted = jnp.dot(
            powers.astype(jnp.bfloat16), value_rows, preferred_element_type=jnp.float32
        )
        return peak, jnp.sum(powers, axis=1, keepdims=True), weighted

    for g in range(groups):
        span = slice(g * head, (g + 1) * head)
        queries = local[:, span]
        scores = lax.dot_general(queries, keys[...], across, preferred_element_type=jnp.float32)
        prefix_peak, prefix_total, prefix_sum = parts(scores * scale, values[...])
        scores = lax.dot_general(queries, new_keys, across, preferred_element_type=jnp.float32)
        new_peak, new_total, new_sum = parts(jnp.where(seen, scores * scale, -1e30), new_values)
        peak = jnp.maximum(prefix_peak, new_peak)
        prefix_factor = jnp.exp(prefix_peak - peak)
        new_factor = jnp.exp(new_peak - peak)
        total = prefix_total * prefix_factor + new_total * new_factor
        attended = (prefix_sum * prefix_factor + new_sum * new_factor) / total
        out[:, span] = attended.astype(jnp.bfloat16)


def attend(local, keys, values, steps, cols):
    vector = pl.BlockSpec(memory_space=pltpu.VMEM)
    return pl.pallas_call(
        functools.partial(attend_kernel, steps),
        out_shape=jax.ShapeDtypeStruct((local.shape[0], cols), jnp.bfloat16),
        in_specs=[vector] * 3,
        out_specs=vector,
        compiler_params=pltpu.CompilerParams(vmem_limit_bytes=40 * 2**20),
        name="attend",
    )(local, keys, values)


def output_kernel(order, place, own, other, totals, out):
    pair = pl.program_id(0)
    y, z_hi = pair // 2, pair % 2
    core, x_here, y_here, z_here = place[0], place[1], place[2], place[3]
    for ref, plane in ((own, core), (other, 1 - core)):
        turn = lambda at: (at - plane) & 3
        apart = lambda here, there: turn(here) ^ turn(there)
        for z_lo in range(2):
            for x in range(4):
                prompt = z_lo * 8 + x * 2 + plane
                dz, dy, dx = apart(z_here, z_hi * 2 + z_lo), apart(y_here, y), apart(x_here, x)
                far = (dz >> 1) * 4 + (dy >> 1) * 2 + (dx >> 1)
                block = ref[dz & 1, dy & 1, dx & 1, far] - totals[prompt, pair]
                for row in range(4):
                    near, which = divmod(row, 2)
                    to = order[(pair * 2 + near) * 32 + prompt * 2 + which]
                    out[near * 32 + to] = block[row * 4 : row * 4 + 4]


def ordered_output(order, place, own, other, totals):
    width = own.shape[-1]
    whole = lambda a: pl.BlockSpec(a.shape, lambda i, *_: (0,) * a.ndim)
    return pl.pallas_call(
        output_kernel,
        out_shape=jax.ShapeDtypeStruct((512, 4, width), jnp.float32),
        grid_spec=pltpu.PrefetchScalarGridSpec(
            num_scalar_prefetch=2,
            grid=(8,),
            in_specs=[whole(own), whole(other), whole(totals)],
            out_specs=pl.BlockSpec((64, 4, width), lambda i, *_: (i, 0, 0)),
        ),
        compiler_params=pltpu.CompilerParams(vmem_limit_bytes=52 * 2**20),
        name="output",
    )(order, place, own, other, totals)


def rms_scale(rows, gain):
    mean_sq = jnp.mean(rows * rows, axis=-1, keepdims=True)
    return rows * lax.rsqrt(mean_sq + 1e-06) * gain


def log_sum(values, axis):
    top = jnp.max(values, axis=axis, keepdims=True)
    return jnp.squeeze(top, axis) + jnp.log(jnp.sum(jnp.exp(values - top), axis=axis))


def spread(values, axis):
    copies = lax.axis_size(axis)
    return lax.all_to_all(
        jnp.broadcast_to(values[None], (copies,) + values.shape), axis, 0, 0, tiled=True
    )


def on_device(
    embedded,
    attn_gain,
    query_weight,
    key_weight,
    value_weight,
    out_weight,
    final_gain,
    head_weight,
    prefix_keys,
    prefix_values,
    sample_prompt,
):
    samples, steps, width = embedded.shape
    rows = samples * steps
    cols = query_weight.shape[1]
    core = lax.axis_index("grp") % 2
    z_hi = lax.axis_index("vocab") % 2
    z = z_hi * 2 + lax.axis_index("grp") // 8
    y = lax.axis_index("vocab") // 2
    x = (lax.axis_index("grp") // 2) % 4
    shares = lax.axis_size("vocab")
    mine = rows // shares
    span = width // shares
    half = width // 2
    other_weight = swap_cores(head_weight)

    own_columns = lax.axis_index("vocab") * span
    sorted_rows, sample_at = front(
        sample_prompt,
        own_columns.reshape(1).astype(jnp.int32),
        embedded,
        attn_gain,
        query_weight,
        key_weight,
        value_weight,
        span,
    )
    local = lax.all_to_all(sorted_rows, "grp", 0, 0, tiled=True)

    attended = attend(local, prefix_keys[0, 0], prefix_values[0, 0], steps, cols)
    attended, other_weight = lax.optimization_barrier((attended, other_weight))
    own_embedded = local[:, -span:].astype(jnp.float32)

    def product(part, attended):
        w = lax.slice_in_dim(out_weight, part * half, (part + 1) * half, axis=1)
        full = jnp.dot(attended, w, preferred_element_type=jnp.float32)
        at = (y * 2 + z_hi) % 4 * span
        chunk = lax.dynamic_slice_in_dim(full, at, span, 1)
        chunk = jnp.where((y * 2 + z_hi) // 4 == part, chunk + own_embedded, chunk)
        return lax.dynamic_update_slice_in_dim(full, chunk, at, 1)

    both = jnp.concatenate([product(0, attended), product(1, attended)], axis=1)
    arrived = lax.all_to_all(both, "vocab", 0, 0, tiled=True)
    hidden = jnp.sum(arrived.reshape(shares, mine, width), axis=0)
    normed = rms_scale(hidden, final_gain).astype(jnp.bfloat16)

    held, taken = meet_gather([normed[:, a:b] for a, b in PIECES])
    logits, other_logits, local_sum = head_logits(held, taken, head_weight, other_weight, mine)
    crossed = swap_cores(other_logits)

    places = jnp.arange(RING, dtype=jnp.int32)
    apart = lambda at: chip_turn(at, core) ^ chip_turn(places, core)
    dz, dy, dx = apart(z)[:, None, None], apart(y)[None, :, None], apart(x)[None, None, :]
    nears = (dz & 1) * 4 + (dy & 1) * 2 + (dx & 1)
    fars = (dz >> 1) * 4 + (dy >> 1) * 2 + (dx >> 1)
    mine_order = (nears * 8 + fars).reshape(64)
    local_sum = jnp.take(local_sum.reshape(64, mine), mine_order, axis=0)
    over_vocab = log_sum(spread(local_sum.reshape(64 * mine), "vocab"), 0)
    sent = jnp.concatenate([over_vocab, sample_at.astype(jnp.float32)])
    over_grp = spread(sent, "grp")
    order = over_grp[:, 64 * mine :].astype(jnp.int32).reshape(-1)
    total = log_sum(over_grp[:, : 64 * mine].reshape(8, 2, 64 * mine), 0)
    total = total.reshape(2, 2, 2, 4, 4, mine).transpose(2, 4, 0, 3, 1, 5)
    return ordered_output(
        order,
        jnp.stack([core, x, y, z]).astype(jnp.int32),
        logits,
        crossed,
        total.reshape(16, 8, mine, 1),
    )


def solution(mesh):
    placed = (
        P("grp", None, None),
        P(),
        P(None, "vocab"),
        P(None, "vocab"),
        P(None, "vocab"),
        P("vocab", None),
        P(),
        P(None, ("grp", "vocab")),
        P("grp", "vocab", None, None),
        P("grp", "vocab", None, None),
        P("grp"),
    )
    return jax.shard_map(
        on_device,
        mesh=mesh,
        in_specs=placed,
        out_specs=P(None, None, ("grp", "vocab")),
        check_vma=False,
    )
```

```python
import functools

import jax
import jax.numpy as jnp
from jax import lax
from jax.experimental import pallas as pl
from jax.experimental.pallas import tpu as pltpu
from jax.sharding import PartitionSpec as P

BOTH = ("grp", "vocab")
RING = 4
PIECES = ((0, 1536), (1536, 3328), (3328, 5120))
ORDERS = ("xyz", "yzx", "zxy")


def place_of(flat):
    grp, vocab = divmod(flat, 8)
    z_lo, rest = divmod(grp, 8)
    x, core = divmod(rest, 2)
    y, z_hi = divmod(vocab, 2)
    return {"x": x, "y": y, "z": z_hi * 2 + z_lo, "core": core}


def flat_of(at):
    grp = (at["z"] % 2) * 8 + at["x"] * 2 + at["core"]
    return grp * 8 + at["y"] * 2 + at["z"] // 2


def chip_turn(at, core):
    return (at - core) % RING


def meet_pairs(axis, bit):
    pairs = []
    for source in range(128):
        at = place_of(source)
        at[axis] = ((chip_turn(at[axis], at["core"]) ^ bit) + at["core"]) % RING
        pairs.append((source, flat_of(at)))
    return pairs


def swap_pairs(axis, distance, size):
    pairs = []
    for source in range(128):
        at = place_of(source)
        at[axis] = (at[axis] + distance) % size
        pairs.append((source, flat_of(at)))
    return pairs


FAR = {axis: meet_pairs(axis, 2) for axis in "xyz"}
NEAR = {axis: meet_pairs(axis, 1) for axis in "xyz"}
CORES = swap_pairs("core", 1, 2)
HALVES = swap_pairs("z", 2, RING)


def swap_cores(block):
    return lax.ppermute(block, BOTH, CORES)


def meet_gather(blocks):
    held = list(blocks)

    def meet(parts, turn):
        pairs = FAR if turn < 3 else NEAR
        return [
            lax.ppermute(part, BOTH, pairs[order[turn % 3]]) for part, order in zip(parts, ORDERS)
        ]

    for turn in range(4):
        held = [jnp.stack(both) for both in zip(held, meet(held, turn))]
    fifth = meet(held, 4)
    sixth = meet(held, 5)
    fifth = list(lax.optimization_barrier(tuple(fifth)))
    return list(zip(held, fifth)), list(zip(sixth, meet(fifth, 5)))


def weight_copies(k, own_w, other_w, weights, sems):
    a, b = PIECES[k]
    half = own_w.shape[1]
    rows = pl.ds(a, b - a)
    return [
        pltpu.make_async_copy(own_w.at[rows], weights[k].at[:, pl.ds(0, half)], sems.at[k, 0]),
        pltpu.make_async_copy(other_w.at[rows], weights[k].at[:, pl.ds(half, half)], sems.at[k, 1]),
    ]


def head_kernel(mark, *refs):
    parts, (own_w, other_w), refs = (refs[0:2], refs[2:4], refs[4:6]), refs[6:8], refs[8:]
    if mark == 0:
        (out,), work = refs[:1], refs[1:]
    else:
        (before, own_out, other_out, sums), work = refs[:4], refs[4:]
    lhs, weights, (total, lhs_sem, w_sem, in_sem, out_sem) = work[0:3], work[3:6], work[6:]
    mine, cols = total.shape[4:]
    half = own_w.shape[1]

    def copies(k):
        room, sem = lhs[k], lhs_sem.at[k]
        moves = []
        for h, part in enumerate(parts[k]):
            if k == 0:
                moves.append((part, room.at[h]))
            elif k == 1:
                moves += [(part.at[:, x], room.at[h, :, :, :, x]) for x in range(2)]
            else:
                moves += [(part.at[:, :, :, z], room.at[:, h, z]) for z in range(2)]
        return [
            pltpu.make_async_copy(source, to, sem.at[i]) for i, (source, to) in enumerate(moves)
        ] + weight_copies(k, own_w, other_w, weights, w_sem)

    def begin(k):
        for copy in copies(k):
            copy.start()

    def product(k):
        for copy in copies(k):
            copy.wait()
        if k < 2:
            begin(k + 1)
        rows = lhs[k][...].reshape(32 * mine, -1)
        fresh = jnp.dot(rows, weights[k][...], preferred_element_type=jnp.float32)
        return fresh.reshape(2, 2, 8, mine, cols)

    def half_rows(k, at):
        rows = lhs[k][at].reshape(16 * mine, -1)
        fresh = jnp.dot(rows, weights[k][...], preferred_element_type=jnp.float32)
        return fresh.reshape(2, 8, mine, cols)

    def arrive(k):
        for copy in copies(k):
            copy.wait()

    begin(0)
    if mark == 0:
        begin(1)
        begin(2)
        arrive(0)
        total[1] = jnp.zeros(total.shape[1:], jnp.float32)

        def first(y, carry):
            total[0, y] = half_rows(0, y)
            return carry

        lax.fori_loop(0, 2, first, 0)
    else:
        load = pltpu.make_async_copy(before, total, in_sem)
        load.start()
        fresh = product(0)
        load.wait()
        total[1] += fresh
    def out_copies(z, y):
        if mark == 0:
            return [pltpu.make_async_copy(total.at[z, y], out.at[z, y], out_sem.at[z, y, 0])]
        return [
            pltpu.make_async_copy(
                total.at[z, y, :, :, :, pl.ds(at * half, half)], ref.at[z, y], out_sem.at[z, y, at]
            )
            for at, ref in enumerate((own_out, other_out))
        ]

    def finish(z, y):
        for copy in out_copies(z, y):
            copy.start()
        if mark == 1:
            rows = total[z, y].reshape(16 * mine, cols)
            top = jnp.max(rows, axis=1, keepdims=True)
            mass = jnp.sum(jnp.exp(rows - top), axis=1, keepdims=True)
            at = pl.ds(pl.multiple_of((z * 2 + y) * 16 * mine, 16 * mine), 16 * mine)
            sums[at] = top + jnp.log(mass)

    if mark == 0:

        def second(z, carry):
            total[z, :, 0] += half_rows(1, z)
            return carry

        def third(z, carry):
            total[z, 0] += half_rows(2, z)
            finish(z, 0)
            finish(z, 1)
            return carry

        arrive(1)
        lax.fori_loop(0, 2, second, 0)
        arrive(2)
        lax.fori_loop(0, 2, third, 0)
    else:
        total[:, :, mark] += product(1)
        for z in range(2):
            finish(z, 1 - mark)
        total[:, mark] += product(2)
        for z in range(2):
            finish(z, mark)
    for z in range(2):
        for y in range(2):
            for copy in out_copies(z, y):
                copy.wait()


def head_logits(held, taken, own_w, other_w, mine):
    half = own_w.shape[1]
    rows = 64 * mine
    anywhere = pl.BlockSpec(memory_space=pl.ANY)
    widths = [b - a for a, b in PIECES]
    shape = (2, 2, 2, 8, mine)
    flops = rows * 5120 * 2 * half

    def call(mark, out_shape, out_specs, operands):
        return pl.pallas_call(
            functools.partial(head_kernel, mark),
            out_shape=out_shape,
            in_specs=[anywhere] * len(operands),
            out_specs=out_specs,
            scratch_shapes=[pltpu.VMEM((2, 2, 2, 2, 2, mine, w), jnp.bfloat16) for w in widths]
            + [pltpu.VMEM((w, 2 * half), jnp.bfloat16) for w in widths]
            + [
                pltpu.VMEM(shape + (2 * half,), jnp.float32),
                pltpu.SemaphoreType.DMA((3, 4)),
                pltpu.SemaphoreType.DMA((3, 2)),
                pltpu.SemaphoreType.DMA,
                pltpu.SemaphoreType.DMA((2, 2, 2)),
            ],
            compiler_params=pltpu.CompilerParams(vmem_limit_bytes=48 * 2**20),
            cost_estimate=pl.CostEstimate(
                flops=flops, bytes_accessed=26 * 10**6, transcendentals=mark * rows * 2 * half
            ),
            name=("head_early", "head_late")[mark],
        )(*operands)

    early = call(
        0,
        jax.ShapeDtypeStruct(shape + (2 * half,), jnp.float32),
        anywhere,
        [half for piece in held for half in piece] + [own_w, other_w],
    )
    return call(
        1,
        (
            jax.ShapeDtypeStruct(shape + (half,), jnp.float32),
            jax.ShapeDtypeStruct(shape + (half,), jnp.float32),
            jax.ShapeDtypeStruct((rows, 1), jnp.float32),
        ),
        (anywhere, anywhere, pl.BlockSpec(memory_space=pltpu.VMEM)),
        [half for piece in taken for half in piece] + [own_w, other_w, early],
    )


def front_kernel(
    prompts, column, embedded, gain, query_w, key_w, value_w, out, order, seen, raw, weights, sems
):
    samples, steps, width = embedded.shape
    cuts = (0, query_w.shape[1], query_w.shape[1] + key_w.shape[1])
    copies = [
        pltpu.make_async_copy(w, weights.at[:, pl.ds(at, w.shape[1])], sems.at[i])
        for i, (w, at) in enumerate(zip((query_w, key_w, value_w), cuts))
    ]
    for copy in copies:
        copy.start()
    for p in range(samples // 2):
        seen[p] = 0
    for i in range(samples):
        p = prompts[i]
        slot = p * 2 + seen[p]
        seen[p] = seen[p] + 1
        order[slot] = i
    for slot in range(samples):
        raw[slot * steps : (slot + 1) * steps] = embedded[order[slot]].astype(jnp.float32)
    rows = raw[...]
    mean_sq = jnp.mean(rows * rows, axis=-1, keepdims=True)
    normed = (rows * lax.rsqrt(mean_sq + 1e-06) * gain[...]).astype(jnp.bfloat16)
    span = out.shape[1] - weights.shape[1]
    at = pl.multiple_of(column[0], 128)
    out[:, weights.shape[1] :] = raw[:, pl.ds(at, span)].astype(jnp.bfloat16)
    for copy in copies:
        copy.wait()
    out[:, : weights.shape[1]] = jnp.dot(
        normed, weights[...], preferred_element_type=jnp.float32
    ).astype(jnp.bfloat16)


def front(sample_prompt, column, embedded, gain, query_w, key_w, value_w, span):
    samples, steps, width = embedded.shape
    anywhere = pl.BlockSpec(memory_space=pl.ANY)
    scalars = pl.BlockSpec(memory_space=pltpu.SMEM)
    vector = pl.BlockSpec(memory_space=pltpu.VMEM)
    cols = query_w.shape[1] + key_w.shape[1] + value_w.shape[1]
    return pl.pallas_call(
        front_kernel,
        out_shape=(
            jax.ShapeDtypeStruct((samples * steps, cols + span), jnp.bfloat16),
            jax.ShapeDtypeStruct((samples,), jnp.int32),
        ),
        in_specs=[scalars, scalars, vector, vector, anywhere, anywhere, anywhere],
        out_specs=(vector, scalars),
        scratch_shapes=[
            pltpu.SMEM((samples // 2,), jnp.int32),
            pltpu.VMEM((samples * steps, width), jnp.float32),
            pltpu.VMEM((width, cols), jnp.bfloat16),
            pltpu.SemaphoreType.DMA((3,)),
        ],
        compiler_params=pltpu.CompilerParams(vmem_limit_bytes=60 * 2**20),
        cost_estimate=pl.CostEstimate(
            flops=2 * samples * steps * width * cols, bytes_accessed=10**7, transcendentals=0
        ),
        name="front",
    )(sample_prompt, column, embedded, gain.reshape(1, -1), query_w, key_w, value_w)


def attend_kernel(steps, local, keys, values, out):
    head = keys.shape[1]
    rows = local.shape[0]
    groups = out.shape[1] // head
    scale = 1.0 / head**0.5
    new_keys = local[:, groups * head : (groups + 1) * head]
    new_values = local[:, (groups + 1) * head : (groups + 2) * head]
    at_row = lax.broadcasted_iota(jnp.int32, (rows, rows), 0)
    at_col = lax.broadcasted_iota(jnp.int32, (rows, rows), 1)
    seen = (at_row // steps == at_col // steps) & (at_col <= at_row)
    across = (((1,), (1,)), ((), ()))

    def parts(scores, value_rows):
        peak = jnp.max(scores, axis=1, keepdims=True)
        powers = jnp.exp(scores - peak)
        weighted = jnp.dot(
            powers.astype(jnp.bfloat16), value_rows, preferred_element_type=jnp.float32
        )
        return peak, jnp.sum(powers, axis=1, keepdims=True), weighted

    for g in range(groups):
        span = slice(g * head, (g + 1) * head)
        queries = local[:, span]
        scores = lax.dot_general(queries, keys[...], across, preferred_element_type=jnp.float32)
        prefix_peak, prefix_total, prefix_sum = parts(scores * scale, values[...])
        scores = lax.dot_general(queries, new_keys, across, preferred_element_type=jnp.float32)
        new_peak, new_total, new_sum = parts(jnp.where(seen, scores * scale, -1e30), new_values)
        peak = jnp.maximum(prefix_peak, new_peak)
        prefix_factor = jnp.exp(prefix_peak - peak)
        new_factor = jnp.exp(new_peak - peak)
        total = prefix_total * prefix_factor + new_total * new_factor
        attended = (prefix_sum * prefix_factor + new_sum * new_factor) / total
        out[:, span] = attended.astype(jnp.bfloat16)


def attend(local, keys, values, steps, cols):
    vector = pl.BlockSpec(memory_space=pltpu.VMEM)
    return pl.pallas_call(
        functools.partial(attend_kernel, steps),
        out_shape=jax.ShapeDtypeStruct((local.shape[0], cols), jnp.bfloat16),
        in_specs=[vector] * 3,
        out_specs=vector,
        compiler_params=pltpu.CompilerParams(vmem_limit_bytes=40 * 2**20),
        name="attend",
    )(local, keys, values)


def output_kernel(order, place, own, other, totals, out):
    pair = pl.program_id(0)
    y, z_hi = pair // 2, pair % 2
    core, x_here, y_here, z_here = place[0], place[1], place[2], place[3]
    for ref, plane in ((own, core), (other, 1 - core)):
        turn = lambda at: (at - plane) & 3
        apart = lambda here, there: turn(here) ^ turn(there)
        for z_lo in range(2):
            for x in range(4):
                prompt = z_lo * 8 + x * 2 + plane
                dz, dy, dx = apart(z_here, z_hi * 2 + z_lo), apart(y_here, y), apart(x_here, x)
                far = (dz >> 1) * 4 + (dy >> 1) * 2 + (dx >> 1)
                block = ref[dz & 1, dy & 1, dx & 1, far] - totals[prompt, pair]
                for row in range(4):
                    near, which = divmod(row, 2)
                    to = order[(pair * 2 + near) * 32 + prompt * 2 + which]
                    out[near * 32 + to] = block[row * 4 : row * 4 + 4]


def ordered_output(order, place, own, other, totals):
    width = own.shape[-1]
    whole = lambda a: pl.BlockSpec(a.shape, lambda i, *_: (0,) * a.ndim)
    return pl.pallas_call(
        output_kernel,
        out_shape=jax.ShapeDtypeStruct((512, 4, width), jnp.float32),
        grid_spec=pltpu.PrefetchScalarGridSpec(
            num_scalar_prefetch=2,
            grid=(8,),
            in_specs=[whole(own), whole(other), whole(totals)],
            out_specs=pl.BlockSpec((64, 4, width), lambda i, *_: (i, 0, 0)),
        ),
        compiler_params=pltpu.CompilerParams(vmem_limit_bytes=52 * 2**20),
        name="output",
    )(order, place, own, other, totals)


def rms_scale(rows, gain):
    mean_sq = jnp.mean(rows * rows, axis=-1, keepdims=True)
    return rows * lax.rsqrt(mean_sq + 1e-06) * gain


def log_sum(values, axis):
    top = jnp.max(values, axis=axis, keepdims=True)
    return jnp.squeeze(top, axis) + jnp.log(jnp.sum(jnp.exp(values - top), axis=axis))


def spread(values, axis):
    copies = lax.axis_size(axis)
    return lax.all_to_all(
        jnp.broadcast_to(values[None], (copies,) + values.shape), axis, 0, 0, tiled=True
    )


def on_device(
    embedded,
    attn_gain,
    query_weight,
    key_weight,
    value_weight,
    out_weight,
    final_gain,
    head_weight,
    prefix_keys,
    prefix_values,
    sample_prompt,
):
    samples, steps, width = embedded.shape
    rows = samples * steps
    cols = query_weight.shape[1]
    core = lax.axis_index("grp") % 2
    z_hi = lax.axis_index("vocab") % 2
    z = z_hi * 2 + lax.axis_index("grp") // 8
    y = lax.axis_index("vocab") // 2
    x = (lax.axis_index("grp") // 2) % 4
    shares = lax.axis_size("vocab")
    mine = rows // shares
    span = width // shares
    half = width // 2
    other_weight = swap_cores(head_weight)

    own_columns = lax.axis_index("vocab") * span
    sorted_rows, sample_at = front(
        sample_prompt,
        own_columns.reshape(1).astype(jnp.int32),
        embedded,
        attn_gain,
        query_weight,
        key_weight,
        value_weight,
        span,
    )
    local = lax.all_to_all(sorted_rows, "grp", 0, 0, tiled=True)

    attended = attend(local, prefix_keys[0, 0], prefix_values[0, 0], steps, cols)
    attended, other_weight = lax.optimization_barrier((attended, other_weight))
    own_embedded = local[:, -span:].astype(jnp.float32)

    def product(part, attended):
        w = lax.slice_in_dim(out_weight, part * half, (part + 1) * half, axis=1)
        full = jnp.dot(attended, w, preferred_element_type=jnp.float32)
        at = (y * 2 + z_hi) % 4 * span
        chunk = lax.dynamic_slice_in_dim(full, at, span, 1)
        chunk = jnp.where((y * 2 + z_hi) // 4 == part, chunk + own_embedded, chunk)
        return lax.dynamic_update_slice_in_dim(full, chunk, at, 1)

    both = jnp.concatenate([product(0, attended), product(1, attended)], axis=1)
    arrived = lax.all_to_all(both, "vocab", 0, 0, tiled=True)
    hidden = jnp.sum(arrived.reshape(shares, mine, width), axis=0)
    normed = rms_scale(hidden, final_gain).astype(jnp.bfloat16)

    held, taken = meet_gather([normed[:, a:b] for a, b in PIECES])
    logits, other_logits, local_sum = head_logits(held, taken, head_weight, other_weight, mine)
    crossed = swap_cores(other_logits)

    places = jnp.arange(RING, dtype=jnp.int32)
    apart = lambda at: chip_turn(at, core) ^ chip_turn(places, core)
    dz, dy, dx = apart(z)[:, None, None], apart(y)[None, :, None], apart(x)[None, None, :]
    nears = (dz & 1) * 4 + (dy & 1) * 2 + (dx & 1)
    fars = (dz >> 1) * 4 + (dy >> 1) * 2 + (dx >> 1)
    mine_order = (nears * 8 + fars).reshape(64)
    local_sum = jnp.take(local_sum.reshape(64, mine), mine_order, axis=0)
    over_vocab = log_sum(spread(local_sum.reshape(64 * mine), "vocab"), 0)
    sent = jnp.concatenate([over_vocab, sample_at.astype(jnp.float32)])
    over_grp = spread(sent, "grp")
    order = over_grp[:, 64 * mine :].astype(jnp.int32).reshape(-1)
    total = log_sum(over_grp[:, : 64 * mine].reshape(8, 2, 64 * mine), 0)
    total = total.reshape(2, 2, 2, 4, 4, mine).transpose(2, 4, 0, 3, 1, 5)
    return ordered_output(
        order,
        jnp.stack([core, x, y, z]).astype(jnp.int32),
        logits,
        crossed,
        total.reshape(16, 8, mine, 1),
    )


def solution(mesh):
    placed = (
        P("grp", None, None),
        P(),
        P(None, "vocab"),
        P(None, "vocab"),
        P(None, "vocab"),
        P("vocab", None),
        P(),
        P(None, ("grp", "vocab")),
        P("grp", "vocab", None, None),
        P("grp", "vocab", None, None),
        P("grp"),
    )
    return jax.shard_map(
        on_device,
        mesh=mesh,
        in_specs=placed,
        out_specs=P(None, None, ("grp", "vocab")),
        check_vma=False,
    )
```
